32 devices in a mesh: scen: 8 (over z, y), link: 4 (over x, core).
Axes of the slice: x: 2, y: 2, z: 4, core: 2. Of those that a mesh axis runs over, the one named last changes fastest.
Arguments:
- factor_inv: bfloat16 [16, 1024, 1024], P('scen'), may hold values from -0.1875 to 0.1875
- coupling: bfloat16 [16, 1024, 1024], P('scen', None, 'link'), may hold values from -0.375 to 0.375
- first_diag: float32 [128, 128], P('scen'), may hold values from 1 to 10
- pattern: int32 [16, 8], P('scen'), may hold values from 0 to 127, as said below
Outputs:
- panel: float32 [16384, 128], P('scen')
- trailing: float32 [16384, 16384], P('scen', 'link')
The draws below stay inside these ranges and needn't reach their ends.
Inputs may be any that keep to these rules, and one draw needn't show every extreme that they name: `pattern`: slot t of a scenario names a block of column range t // 2, that is, a block p with p // 32 = t // 2. The 2 scenarios of rows s * 2 to (s + 1) * 2 - 1 name every block at most once among them, and at most 2 blocks of any one group of blocks with the same p // 16. The first scenario of every such set names block 0 in slot 0.
All inputs are finite; a program needn't handle non-finite values.
Results may differ from the reference program's by a relative error of at most 0.0005.
Values may be sent and summed in bfloat16 or wider, within the bound.
A program may use at most 128 MiB of HBM per device.

```python
import math
import jax
import jax.numpy as jnp
from jax import lax

NB = 128
TILE = 128
NS = 1024
KL = 2
S_DEV = 2
KB = 8
SCENARIOS = 16
N_SCEN = 8
N_LINK = 4


def draw_pattern(key, part):
    per_range = NB // N_LINK
    owner_rows = NB // N_SCEN
    picks = S_DEV * KL
    owners_here = per_range // owner_rows
    limit = max(1, (picks + owners_here - 1) // owners_here)
    key_pop, key_noise = jax.random.split(jax.random.fold_in(key, 7))
    popular = jax.random.randint(key_pop, (N_LINK, per_range), 0, 4)
    noise = jax.random.randint(key_noise, (N_SCEN, N_LINK, per_range), 0, 65536)
    position = lax.broadcasted_iota(jnp.int32, (N_SCEN, N_LINK, per_range), 2)
    range_pos = lax.broadcasted_iota(jnp.int32, (N_SCEN, N_LINK, per_range), 1)
    leading = ((position == 0) & (range_pos == 0)).astype(jnp.int32) * 16777216
    scores = (popular[None, :, :] * 65536 + noise) * per_range + position + leading
    grouped = scores.reshape(N_SCEN, N_LINK, owners_here, owner_rows)
    above = jnp.sum((grouped[:, :, :, None, :] > grouped[:, :, :, :, None]).astype(jnp.int32), axis=4)
    allowed = (above < limit).astype(jnp.int32).reshape(N_SCEN, N_LINK, per_range)
    final = allowed * 67108864 + scores
    order = jnp.argsort(-final, axis=2, stable=True)
    chosen = order[:, :, :picks].reshape(N_SCEN, N_LINK, S_DEV, KL).transpose(0, 2, 1, 3)
    offsets = (jnp.arange(N_LINK, dtype=jnp.int32) * per_range)[None, None, :, None]
    return (chosen + offsets).reshape(N_SCEN * S_DEV, N_LINK * KL).astype(jnp.int32)


def draw_coupling(key, part):
    key_own, key_common = jax.random.split(jax.random.fold_in(key, 11))
    own = jnp.clip(jax.random.normal(key_own, (SCENARIOS, NS, KB * TILE), jnp.float32), -6.0, 6.0)
    common = jnp.clip(jax.random.normal(key_common, (SCENARIOS, NS, 1), jnp.float32), -6.0, 6.0)
    return ((own + common) * NS ** (-0.5)).astype(jnp.bfloat16)


def levels(key, dims, shards, smallest, high):
    gain, own = 1.0, jax.random.fold_in(key, 6)
    for dim, parts in shards:
        heights = jnp.exp(jax.random.uniform(jax.random.fold_in(own, dim), (parts,), jnp.float32, smallest / len(shards), high / len(shards)))
        gain = gain * jnp.repeat(heights, dims[dim] // parts).reshape([-1 if axis == dim else 1 for axis in range(len(dims))])
    return gain


def scatter_about(stream_key, dims, scale, reach, shards=(), held_as=jnp.bfloat16):
    factor_of = levels(stream_key, dims, shards, -0.22, 0.18) if shards else 1.0
    entries = jax.random.normal(stream_key, dims, jnp.float32) * scale * factor_of
    return jnp.minimum(jnp.maximum(entries, -reach), reach).astype(held_as)


def setup_inputs(seed: int = 0) -> dict:
    splits = jax.random.split(jax.random.key(seed), 5)
    return {
        "factor_inv": scatter_about(splits[0], (SCENARIOS, NS, NS), NS ** -0.5, 0.1875, ((0, 8),)),
        "coupling": draw_coupling(jax.random.fold_in(splits[4], 71), 0),
        "first_diag": jnp.clip(jnp.exp(math.log(10.0) - 2.3025851 * jax.random.uniform(splits[2], (NB, TILE), jnp.float32) ** levels(splits[2], (NB, TILE), ((0, 8),), -0.2, 0.2)), 1.0, 10.0),
        "pattern": draw_pattern(jax.random.fold_in(splits[4], 71), 0),
    }


def reference(factor_inv, coupling, first_diag, pattern):

    def add_scenario(tiles, inputs):
        factor, columns, picked = inputs
        slabs = jnp.dot(factor.astype(jnp.float32), columns.astype(jnp.float32), preferred_element_type=jnp.float32).astype(jnp.bfloat16)
        gram = jnp.dot(slabs.T.astype(jnp.float32), slabs.astype(jnp.float32), preferred_element_type=jnp.float32)
        gram_tiles = gram.reshape(KB, TILE, KB, TILE).transpose(0, 2, 1, 3)
        picked = picked.astype(jnp.int32)
        return (tiles.at[picked[:, None], picked[None, :]].add(gram_tiles), None)
    empty = jnp.zeros((NB, NB, TILE, TILE), jnp.float32)
    tiles, unused = lax.scan(add_scenario, empty, (factor_inv, coupling, pattern))
    diag_tiles = first_diag[:, :, None] * jnp.eye(TILE, dtype=jnp.float32)[None, :, :]
    span = jnp.arange(NB, dtype=jnp.int32)
    tiles = tiles.at[span, span].add(diag_tiles)
    schur = tiles.transpose(0, 2, 1, 3).reshape(NB * TILE, NB * TILE)
    lead_factor = jnp.linalg.cholesky(schur[:TILE, :TILE])
    solved = jax.scipy.linalg.solve_triangular(lead_factor, schur[:, :TILE].T, lower=True).T
    panel = jnp.concatenate([lead_factor, solved[TILE:]], axis=0)
    trailing = schur - jnp.dot(panel.astype(jnp.float32), panel.T.astype(jnp.float32), precision=lax.Precision.HIGHEST, preferred_element_type=jnp.float32)
    return (panel, trailing)
```

```python
import functools

import jax
import jax.numpy as jnp
from jax import lax
from jax.experimental import pallas as pl
from jax.experimental.pallas import tpu as pltpu
from jax.sharding import PartitionSpec as P

F32 = jnp.float32
BF16 = jnp.bfloat16
HIGHEST = lax.Precision.HIGHEST


def factor(work):
    size = work.shape[0]
    inverse = (
        lax.broadcasted_iota(jnp.int32, (size, size), 0)
        == lax.broadcasted_iota(jnp.int32, (size, size), 1)
    ).astype(F32)
    upper_rows, inverse_rows = [], []
    base = 0
    for j in range(size):
        start = j // 8 * 8
        if start > base:
            work, inverse, base = work[start - base :], inverse[start - base :], start
        k = j - base
        column = work[:, j : j + 1]
        pivot = column[k : k + 1]
        row, inverse_row = work[k : k + 1], inverse[k : k + 1]
        scale = 1.0 / jnp.sqrt(pivot)
        upper_rows.append(row * scale)
        inverse_rows.append(inverse_row * scale)
        if j + 1 < size:
            below = lax.broadcasted_iota(jnp.int32, (size - base, 1), 0) > k
            ratio = jnp.where(below, column * (1.0 / pivot), 0.0)
            work = work - ratio * row
            inverse = inverse - ratio * inverse_row
    return jnp.concatenate(upper_rows, axis=0), jnp.concatenate(inverse_rows, axis=0)


def factor_kernel(corner_ref, lower_ref, inverse_ref):
    upper, inverse = factor(corner_ref[...])
    size = upper.shape[0]
    keep = lax.broadcasted_iota(jnp.int32, (size, size), 0) <= lax.broadcasted_iota(
        jnp.int32, (size, size), 1
    )
    lower_ref[...] = jnp.where(keep, upper, 0.0).T
    inverse_ref[...] = inverse


def lead_factor(corner):
    size = corner.shape[0]
    shape = jax.ShapeDtypeStruct((size, size), F32)
    return pl.pallas_call(
        factor_kernel,
        out_shape=(shape, shape),
        name="lead_factor",
        compiler_params=pltpu.CompilerParams(vmem_limit_bytes=32 * 2**20),
    )(corner)


def split(value):
    high = value.astype(BF16)
    return high, (value - high.astype(F32)).astype(BF16)


def finish_kernel(
    place_ref,
    row_label_ref,
    col_label_ref,
    lead_label_ref,
    arrived_ref,
    lead_ref,
    column_ref,
    lower_ref,
    inverse_ref,
    diag_ref,
    panel_ref,
    trailing_ref,
    partner_ref,
    raw_ref,
):
    tile = lower_ref.shape[0]
    width = trailing_ref.shape[1]
    slots = arrived_ref.shape[2] // tile
    row = pl.program_id(0)
    rows_own = pl.num_programs(0)
    global_row = place_ref[0] * rows_own + row
    first_col = place_ref[1] * (width // tile)
    chunk = 512

    @pl.when(row == 0)
    def _():
        raw_ref[...] = jnp.zeros_like(raw_ref)
        for source in range(lead_ref.shape[0]):
            for slot in range(slots):
                at = pl.multiple_of(lead_label_ref[source * slots + slot] * tile, tile)
                raw_ref[:, pl.ds(at, tile)] += lead_ref[source, :, slot * tile : (slot + 1) * tile]

        @pl.loop(0, width // chunk)
        def _(step):
            at = pl.ds(pl.multiple_of(step * chunk, chunk), chunk)
            high, low = split(
                jnp.dot(
                    inverse_ref[...], raw_ref[:, at], precision=HIGHEST, preferred_element_type=F32
                )
            )
            partner_ref[:tile, at] = high
            partner_ref[tile : 2 * tile, at] = high
            partner_ref[2 * tile :, at] = low

        @pl.when(first_col == 0)
        def _():
            high, low = split(lower_ref[...].T)
            partner_ref[:tile, :tile] = high
            partner_ref[tile : 2 * tile, :tile] = high
            partner_ref[2 * tile :, :tile] = low

    solved = lax.dot_general(
        column_ref[...],
        inverse_ref[...],
        (((1,), (1,)), ((), ())),
        precision=HIGHEST,
        preferred_element_type=F32,
    )
    mine = jnp.where(global_row == 0, lower_ref[...], solved)
    panel_ref[...] = mine
    high, low = split(-mine)
    left = jnp.concatenate([high, low, high], axis=1)
    for step in range(width // chunk):
        at = slice(step * chunk, (step + 1) * chunk)
        trailing_ref[:, at] = jnp.dot(left, partner_ref[:, at], preferred_element_type=F32)

    @pl.loop(0, arrived_ref.shape[0])
    def _(listed):
        @pl.when(row_label_ref[listed] == row)
        def _():
            for slot in range(slots):
                at = pl.multiple_of(col_label_ref[listed * slots + slot] * tile, tile)
                trailing_ref[:, pl.ds(at, tile)] += arrived_ref[
                    listed, :, slot * tile : (slot + 1) * tile
                ]

    on_col = global_row - first_col

    @pl.when((on_col >= 0) & (on_col < width // tile))
    def _():
        at = pl.multiple_of(on_col * tile, tile)
        unit = lax.broadcasted_iota(jnp.int32, (tile, tile), 0) == lax.broadcasted_iota(
            jnp.int32, (tile, tile), 1
        )
        trailing_ref[:, pl.ds(at, tile)] += jnp.where(unit, diag_ref[pl.ds(row, 1), :], 0.0)


def finish(place, row_labels, col_labels, lead_labels, arrived, lead, column, lower, inverse, diag, width):
    tile = lower.shape[0]
    rows_own = diag.shape[0]
    whole = pl.BlockSpec(memory_space=pltpu.VMEM)
    return pl.pallas_call(
        finish_kernel,
        grid_spec=pltpu.PrefetchScalarGridSpec(
            num_scalar_prefetch=4,
            grid=(rows_own,),
            in_specs=[
                whole,
                whole,
                pl.BlockSpec((tile, tile), lambda r, *_: (r, 0)),
                whole,
                whole,
                whole,
            ],
            out_specs=[
                pl.BlockSpec((tile, tile), lambda r, *_: (r, 0)),
                pl.BlockSpec((tile, width), lambda r, *_: (r, 0)),
            ],
            scratch_shapes=[pltpu.VMEM((3 * tile, width), BF16), pltpu.VMEM((tile, width), F32)],
        ),
        out_shape=(
            jax.ShapeDtypeStruct((rows_own * tile, tile), F32),
            jax.ShapeDtypeStruct((rows_own * tile, width), F32),
        ),
        name="finish",
        compiler_params=pltpu.CompilerParams(vmem_limit_bytes=48 * 2**20),
    )(place, row_labels, col_labels, lead_labels, arrived, lead, column, lower, inverse, diag)


def per_device(factor_inv, coupling, first_diag, pattern):
    rows_own, tile = first_diag.shape
    scen_count = lax.axis_size("scen")
    link_count = lax.axis_size("link")
    scen_pos = lax.axis_index("scen")
    link_pos = lax.axis_index("link")
    per_link = rows_own * scen_count // link_count
    scen_here, spread = pattern.shape
    width = coupling.shape[2]
    slots = width // tile

    own = jnp.einsum("snm,smc->snc", factor_inv, coupling, preferred_element_type=F32).astype(BF16)
    patterns = lax.all_gather(pattern, "scen", axis=0, tiled=False)

    share = lax.dot_general(
        own[0, :, :tile], own[0, :, :tile], (((0,), (0,)), ((), ())), preferred_element_type=F32
    )
    unit = jnp.eye(tile, dtype=F32)
    share = share + jnp.where(scen_pos == 0, first_diag[0][:, None] * unit, 0.0)
    corner = lax.psum(jnp.where(link_pos == 0, share, 0.0), ("scen", "link"))
    lower, inverse = lead_factor(corner)

    contrib = jnp.einsum(
        "snr,snc->src",
        lax.all_gather(own, "link", axis=2, tiled=True),
        own,
        preferred_element_type=F32,
    ).reshape(scen_here * spread, tile, width)

    picks = scen_here * slots
    owners_here = per_link // rows_own if per_link >= rows_own else 1
    limit = max(1, (picks + owners_here - 1) // owners_here)
    listed = jnp.arange(scen_here * spread, dtype=jnp.int32)
    blocks = patterns.reshape(scen_count, scen_here * spread)
    owners = blocks // rows_own
    earlier = (owners[:, :, None] == owners[:, None, :]) & (listed[None, :] < listed[:, None])
    rank = jnp.sum(earlier.astype(jnp.int32), axis=2)
    target = owners * limit + rank
    places = jnp.arange(scen_count * limit, dtype=jnp.int32)
    hit = target[:, :, None] == places[None, None, :]
    at_place = jnp.sum(jnp.where(hit, listed[None, :, None] + 1, 0), axis=1) - 1
    mine = lax.dynamic_index_in_dim(at_place, scen_pos, 0, keepdims=False)
    outgoing = contrib[jnp.maximum(mine, 0)]
    to_me = lax.dynamic_slice_in_dim(at_place, scen_pos * limit, limit, 1)
    chosen = jnp.maximum(to_me, 0)
    block_here = jnp.take_along_axis(blocks, chosen, axis=1)
    row_labels = jnp.where(to_me >= 0, block_here - scen_pos * rows_own, -1).reshape(-1)
    own_cols = (
        lax.dynamic_slice_in_dim(patterns, link_pos * slots, slots, 2) - link_pos * per_link
    )
    col_labels = jnp.take_along_axis(own_cols, (chosen // spread)[:, :, None], axis=1).reshape(-1)
    lead_labels = own_cols[:, 0, :].reshape(-1)

    arrived = lax.all_to_all(outgoing, "scen", split_axis=0, concat_axis=0, tiled=True)
    lead = lax.all_gather(contrib[0], "scen", axis=0, tiled=False)

    first_col = col_labels.reshape(-1, slots)[:, 0] == 0
    pick = (
        (row_labels[:, None] == jnp.arange(rows_own, dtype=jnp.int32)[None, :])
        & first_col[:, None]
        & (link_pos == 0)
    )
    spot = jnp.sum(pick.astype(jnp.int32), axis=0)
    column = jnp.einsum(
        "nr,nxy->rxy", pick.astype(F32), arrived[:, :, :tile], precision=HIGHEST
    ).reshape(rows_own * tile, tile)
    del spot
    column = lax.psum(column, "link")

    place = jnp.stack([scen_pos, link_pos]).astype(jnp.int32)
    return finish(
        place, row_labels, col_labels, lead_labels, arrived, lead, column, lower, inverse, first_diag,
        per_link * tile,
    )


def solution(mesh):
    in_specs = (P("scen", None, None), P("scen", None, "link"), P("scen", None), P("scen", None))
    out_specs = (P("scen", None), P("scen", "link"))
    return jax.shard_map(
        per_device, mesh=mesh, in_specs=in_specs, out_specs=out_specs, check_vma=False
    )
```

```python
import jax
import jax.numpy as jnp
from jax import lax
from jax.experimental import pallas as pl
from jax.experimental.pallas import tpu as pltpu
from jax.sharding import PartitionSpec as P

F32 = jnp.float32
BF16 = jnp.bfloat16
I32 = jnp.int32
I16 = jnp.int16
HIGHEST = lax.Precision.HIGHEST
MESH = pl.DeviceIdType.MESH
VMEM = pl.BlockSpec(memory_space=pltpu.VMEM)
SMEM = pl.BlockSpec(memory_space=pltpu.SMEM)
MIB = 2**20
LEVELS = 32767.0


def factor(work):
    size = work.shape[0]
    inverse = (
        lax.broadcasted_iota(I32, (size, size), 0) == lax.broadcasted_iota(I32, (size, size), 1)
    ).astype(F32)
    upper_rows, inverse_rows = [], []
    base = 0
    for j in range(size):
        start = j // 8 * 8
        if start > base:
            work, inverse, base = work[start - base :], inverse[start - base :], start
        k = j - base
        column = work[:, j : j + 1]
        pivot = column[k : k + 1]
        row, inverse_row = work[k : k + 1], inverse[k : k + 1]
        scale = 1.0 / jnp.sqrt(pivot)
        upper_rows.append(row * scale)
        inverse_rows.append(inverse_row * scale)
        if j + 1 < size:
            below = lax.broadcasted_iota(I32, (size - base, 1), 0) > k
            ratio = jnp.where(below, column * (1.0 / pivot), 0.0)
            work = work - ratio * row
            inverse = inverse - ratio * inverse_row
    return jnp.concatenate(upper_rows, axis=0), jnp.concatenate(inverse_rows, axis=0)


def factor_kernel(corner_ref, lower_ref, inverse_ref):
    upper, inverse = factor(corner_ref[...])
    size = upper.shape[0]
    keep = lax.broadcasted_iota(I32, (size, size), 0) <= lax.broadcasted_iota(
        I32, (size, size), 1
    )
    lower_ref[...] = jnp.where(keep, upper, 0.0).T
    inverse_ref[...] = inverse


def lead_factor(corner):
    shape = jax.ShapeDtypeStruct(corner.shape, F32)
    return pl.pallas_call(
        factor_kernel,
        out_shape=(shape, shape),
        in_specs=[VMEM],
        out_specs=(VMEM, VMEM),
        name="lead_factor",
        cost_estimate=pl.CostEstimate(flops=10**10, bytes_accessed=2 * 10**5, transcendentals=0),
        compiler_params=pltpu.CompilerParams(vmem_limit_bytes=16 * MIB),
    )(corner)


def greet(scen_count, link_count):
    scen, link = lax.axis_index("scen"), lax.axis_index("link")
    barrier = pltpu.get_barrier_semaphore()

    @pl.loop(1, scen_count)
    def _(step):
        pl.semaphore_signal(
            barrier,
            inc=1,
            device_id={"scen": lax.rem(scen + step, scen_count)},
            device_id_type=MESH,
        )

    for step in range(1, link_count):
        pl.semaphore_signal(
            barrier,
            inc=1,
            device_id={"link": lax.rem(link + step, link_count)},
            device_id_type=MESH,
        )
    pl.semaphore_wait(barrier, scen_count + link_count - 2)


def corner_kernel(
    scen_count,
    link_count,
    share_ref,
    pattern_ref,
    corner_ref,
    patterns_ref,
    shares_ref,
    send_sem,
    recv_sem,
    link_send,
    link_recv,
    local_sem,
):
    scen, link = lax.axis_index("scen"), lax.axis_index("link")
    greet(scen_count, link_count)

    def share_copy(source, peer):
        return pltpu.make_async_remote_copy(
            src_ref=share_ref,
            dst_ref=shares_ref.at[source],
            send_sem=send_sem.at[0, peer],
            recv_sem=recv_sem.at[0, source],
            device_id={"scen": peer},
            device_id_type=MESH,
        )

    def pattern_copy(source, peer):
        return pltpu.make_async_remote_copy(
            src_ref=pattern_ref,
            dst_ref=patterns_ref.at[source],
            send_sem=send_sem.at[1, peer],
            recv_sem=recv_sem.at[1, source],
            device_id={"scen": peer},
            device_id_type=MESH,
        )

    def corner_copy(target):
        return pltpu.make_async_remote_copy(
            src_ref=corner_ref,
            dst_ref=corner_ref,
            send_sem=link_send.at[target],
            recv_sem=link_recv,
            device_id={"link": target},
            device_id_type=MESH,
        )

    @pl.when(link == 0)
    def _():
        @pl.loop(1, scen_count)
        def _(step):
            share_copy(scen, lax.rem(scen + step, scen_count)).start()

    @pl.loop(1, scen_count)
    def _(step):
        pattern_copy(scen, lax.rem(scen + step, scen_count)).start()

    own = pltpu.make_async_copy(pattern_ref, patterns_ref.at[scen], local_sem.at[0])
    own.start()

    @pl.when(link == 0)
    def _():
        kept = pltpu.make_async_copy(share_ref, shares_ref.at[scen], local_sem.at[1])
        kept.start()
        kept.wait()

        @pl.loop(1, scen_count)
        def _(step):
            peer = lax.rem(scen + step, scen_count)
            share_copy(peer, peer).wait_recv()

        corner_ref[...] = shares_ref[0]

        @pl.loop(1, scen_count)
        def _(source):
            corner_ref[...] += shares_ref[source]

        for target in range(1, link_count):
            corner_copy(target).start()

        @pl.loop(1, scen_count)
        def _(step):
            share_copy(scen, lax.rem(scen + step, scen_count)).wait_send()

        for target in range(1, link_count):
            corner_copy(target).wait_send()

    own.wait()

    @pl.loop(1, scen_count)
    def _(step):
        peer = lax.rem(scen + step, scen_count)
        pattern_copy(peer, peer).wait()

    @pl.when(link != 0)
    def _():
        corner_copy(0).wait_recv()


def sum_corner(share, pattern, scen_count, link_count):
    tile = share.shape[0]
    dma = pltpu.SemaphoreType.DMA
    return pl.pallas_call(
        lambda *refs: corner_kernel(scen_count, link_count, *refs),
        out_shape=(
            jax.ShapeDtypeStruct((tile, tile), F32),
            jax.ShapeDtypeStruct((scen_count,) + pattern.shape, I32),
        ),
        in_specs=[VMEM, VMEM],
        out_specs=(VMEM, VMEM),
        scratch_shapes=[
            pltpu.VMEM((scen_count, tile, tile), F32),
            dma((2, scen_count)),
            dma((2, scen_count)),
            dma((link_count,)),
            dma,
            dma((2,)),
        ],
        name="sum_corner",
        cost_estimate=pl.CostEstimate(flops=8 * 10**9, bytes_accessed=10**6, transcendentals=0),
        compiler_params=pltpu.CompilerParams(
            collective_id=0, has_side_effects=True, vmem_limit_bytes=16 * MIB
        ),
    )(share, pattern)


def contribute_kernel(limit, clear, target_ref, rows_ref, own_ref, coded_ref, scales_ref):
    scenario, piece = pl.program_id(0), pl.program_id(1)
    tile = coded_ref.shape[3]
    slots = coded_ref.shape[1]
    spread = slots * pl.num_programs(1)
    if clear:

        @pl.when((scenario == 0) & (piece == 0))
        def _():
            coded_ref[...] = jnp.zeros_like(coded_ref)
            scales_ref[...] = jnp.zeros_like(scales_ref)

    product = lax.dot_general(
        rows_ref[0, 0], own_ref[0], (((0,), (0,)), ((), ())), preferred_element_type=F32
    )
    for slab in range(slots):
        values = product[slab * tile : (slab + 1) * tile]
        target = target_ref[scenario * spread + piece * slots + slab]
        dest = target // limit
        rank = target - dest * limit
        peak = jnp.max(jnp.abs(values), axis=0, keepdims=True)
        gain = jnp.where(peak > 1e-30, LEVELS / jnp.maximum(peak, 1e-30), 0.0)
        code = jnp.round(values * gain).astype(I32).astype(I16)
        scales_ref[dest, pl.ds(rank, 1), :] = peak * (1.0 / LEVELS)
        for slot in range(slots):
            coded_ref[dest, slot, pl.ds(pl.multiple_of(rank * tile, tile), tile), :] = code[
                :, slot * tile : (slot + 1) * tile
            ]


def contribute(target, gathered, own, tile, scen_count, limit):
    link_count, scen_here, depth, width = gathered.shape
    slots = width // tile
    clear = scen_count * limit > target.shape[0]
    return pl.pallas_call(
        lambda *refs: contribute_kernel(limit, clear, *refs),
        grid_spec=pltpu.PrefetchScalarGridSpec(
            num_scalar_prefetch=1,
            grid=(scen_here, link_count),
            in_specs=[
                pl.BlockSpec((1, 1, depth, width), lambda i, j, _: (j, i, 0, 0)),
                pl.BlockSpec((1, depth, width), lambda i, j, _: (i, 0, 0)),
            ],
            out_specs=[
                pl.BlockSpec((scen_count, slots, limit * tile, tile), lambda i, j, _: (0, 0, 0, 0)),
                pl.BlockSpec((scen_count, 8, width), lambda i, j, _: (0, 0, 0)),
            ],
        ),
        out_shape=(
            jax.ShapeDtypeStruct((scen_count, slots, limit * tile, tile), I16),
            jax.ShapeDtypeStruct((scen_count, 8, width), F32),
        ),
        name="contribute",
        compiler_params=pltpu.CompilerParams(vmem_limit_bytes=40 * MIB),
    )(target, gathered, own)


def exchange_kernel(
    scen_count,
    link_count,
    limit,
    weight_ref,
    coded_ref,
    scales_ref,
    arrived_ref,
    arrived_scales_ref,
    lead_ref,
    lead_scales_ref,
    column_ref,
    wide_ref,
    send_sem,
    recv_sem,
    local_sem,
    link_send,
    link_recv,
):
    scen, link = lax.axis_index("scen"), lax.axis_index("link")
    tile = coded_ref.shape[3]
    slots = coded_ref.shape[1]
    rows_own = column_ref.shape[0] // tile
    chunks = link_recv.shape[0]
    greet(scen_count, link_count)

    def parts(kind, dest):
        if kind == 0:
            return scales_ref.at[dest], arrived_scales_ref
        if kind <= slots:
            return coded_ref.at[dest, kind - 1], None
        if kind == slots + 1:
            return coded_ref.at[0, :, pl.ds(0, tile), :], lead_ref
        return scales_ref.at[0], lead_scales_ref

    def ends(kind, source, dest):
        src, into = parts(kind, dest)
        dst = arrived_ref.at[source, kind - 1] if into is None else into.at[source]
        return src, dst

    def copy(kind, source, peer):
        src, dst = ends(kind, source, peer)
        return pltpu.make_async_remote_copy(
            src_ref=src,
            dst_ref=dst,
            send_sem=send_sem.at[kind, peer],
            recv_sem=recv_sem.at[kind, source],
            device_id={"scen": peer},
            device_id_type=MESH,
        )

    def keep(kind):
        src, dst = ends(kind, scen, scen)
        return pltpu.make_async_copy(src, dst, local_sem.at[kind])

    def over_peers(act):
        @pl.loop(1, scen_count)
        def _(step):
            act(lax.rem(scen + step, scen_count))

    first, later = (0, 1), tuple(range(2, slots + 3))

    def start_first(peer):
        for kind in first:
            copy(kind, scen, peer).start()

    def start_later(peer):
        for kind in later:
            copy(kind, scen, peer).start()

    def finish_send(kinds):
        def act(peer):
            for kind in kinds:
                copy(kind, scen, peer).wait_send()

        return act

    def finish_recv(kinds):
        def act(peer):
            for kind in kinds:
                copy(kind, peer, peer).wait_recv()

        return act

    over_peers(start_first)
    for kind in first + later:
        keep(kind).start()
    over_peers(finish_send(first))
    over_peers(start_later)
    over_peers(finish_recv(first))
    for kind in first + later:
        keep(kind).wait()

    rows = column_ref.shape[0] // chunks

    def column_copy(piece, target, kind):
        at = pl.ds(piece * rows, rows)
        return pltpu.make_async_remote_copy(
            src_ref=column_ref.at[at],
            dst_ref=column_ref.at[at],
            send_sem=link_send.at[kind, piece],
            recv_sem=link_recv.at[piece],
            device_id={"link": target},
            device_id_type=MESH,
        )

    half = link_count // 2

    @pl.when(link == 0)
    def _():
        @pl.loop(0, scen_count)
        def _(source):
            for rank in range(limit):
                at = slice(rank * tile, (rank + 1) * tile)
                wide_ref[source * limit + rank] = (
                    arrived_ref[source, 0, at, :].astype(I32).astype(F32)
                    * arrived_scales_ref[source, rank : rank + 1, :tile]
                )

        per_chunk = rows_own // chunks
        for piece in range(chunks):
            for inner in range(per_chunk):
                block = piece * per_chunk + inner

                def add(listed, total, block=block):
                    return total + weight_ref[block, listed] * wide_ref[listed]

                column_ref[block * tile : (block + 1) * tile, :] = lax.fori_loop(
                    0, scen_count * limit, add, jnp.zeros((tile, tile), F32), unroll=4
                )
            column_copy(piece, half, 0).start()
            for target in range(1, half):
                column_copy(piece, target, target).start()
        for piece in range(chunks):
            for kind in range(half):
                column_copy(piece, half, kind).wait_send()

    @pl.when(link != 0)
    def _():
        for piece in range(chunks):
            column_copy(piece, 0, 0).wait_recv()

            @pl.when(link == half)
            def _():
                for target in range(half + 1, link_count):
                    column_copy(piece, target, target - half).start()

        @pl.when(link == half)
        def _():
            for piece in range(chunks):
                for kind in range(1, half):
                    column_copy(piece, half + 1, kind).wait_send()

    over_peers(finish_recv(later))
    over_peers(finish_send(later))


def exchange(weight, coded, scales, tile, limit, link_count):
    scen_count, slots = coded.shape[:2]
    rows_own = weight.shape[0]
    kinds = slots + 3
    chunks = min(4, rows_own)
    dma = pltpu.SemaphoreType.DMA
    return pl.pallas_call(
        lambda *refs: exchange_kernel(scen_count, link_count, limit, *refs),
        out_shape=(
            jax.ShapeDtypeStruct(coded.shape, I16),
            jax.ShapeDtypeStruct(scales.shape, F32),
            jax.ShapeDtypeStruct((scen_count, slots, tile, tile), I16),
            jax.ShapeDtypeStruct(scales.shape, F32),
            jax.ShapeDtypeStruct((rows_own * tile, tile), F32),
        ),
        in_specs=[SMEM, VMEM, VMEM],
        out_specs=(VMEM,) * 5,
        scratch_shapes=[
            pltpu.VMEM((scen_count * limit, tile, tile), F32),
            dma((kinds, scen_count)),
            dma((kinds, scen_count)),
            dma((kinds,)),
            dma((max(1, link_count // 2), chunks)),
            dma((chunks,)),
        ],
        name="exchange",
        compiler_params=pltpu.CompilerParams(
            collective_id=1, has_side_effects=True, vmem_limit_bytes=48 * MIB
        ),
    )(weight, coded, scales)


def split(value):
    high = value.astype(BF16)
    return high, (value - high.astype(F32)).astype(BF16)


def finish_kernel(
    limit,
    place_ref,
    row_label_ref,
    col_label_ref,
    lead_label_ref,
    arrived_ref,
    scales_ref,
    lead_ref,
    lead_scales_ref,
    column_ref,
    lower_ref,
    inverse_ref,
    diag_ref,
    panel_ref,
    trailing_ref,
    left_ref,
    raw_ref,
):
    tile = lower_ref.shape[0]
    chunk = trailing_ref.shape[1]
    slots = arrived_ref.shape[1]
    rows_own = diag_ref.shape[0]
    step = pl.program_id(0)
    per_chunk = chunk // tile
    scen, link = place_ref[0], place_ref[1]
    first_col = link * per_chunk * pl.num_programs(0)

    @pl.when(step == 0)
    def _():
        raw_ref[...] = jnp.zeros_like(raw_ref)

        @pl.loop(0, lead_ref.shape[0])
        def _(source):
            for slot in range(slots):
                at = pl.multiple_of(lead_label_ref[source * slots + slot] * tile, tile)
                raw_ref[:, pl.ds(at, tile)] += (
                    lead_ref[source, slot].astype(I32).astype(F32)
                    * lead_scales_ref[source, 0:1, slot * tile : (slot + 1) * tile]
                )

        @pl.loop(0, rows_own)
        def _(row):
            at = pl.ds(pl.multiple_of(row * tile, tile), tile)
            solved = lax.dot_general(
                column_ref[at, :],
                inverse_ref[...],
                (((1,), (1,)), ((), ())),
                precision=HIGHEST,
                preferred_element_type=F32,
            )
            mine = jnp.where((scen == 0) & (row == 0), lower_ref[...], solved)
            panel_ref[at, :] = mine
            high, low = split(-mine)
            left_ref[at, :tile] = high
            left_ref[at, tile : 2 * tile] = low
            left_ref[at, 2 * tile :] = high

    part = jnp.dot(
        inverse_ref[...],
        raw_ref[:, pl.ds(pl.multiple_of(step * chunk, chunk), chunk)],
        precision=HIGHEST,
        preferred_element_type=F32,
    )
    is_lead = (link == 0) & (step == 0)
    top = jnp.where(is_lead, lower_ref[...].T, part[:, :tile])
    part = jnp.concatenate([top, part[:, tile:]], axis=1) if per_chunk > 1 else top
    high, low = split(part)
    right = jnp.concatenate([high, high, low], axis=0)
    strip = 2 * tile if rows_own % 2 == 0 else tile
    for at in range(0, rows_own * tile, strip):
        trailing_ref[at : at + strip, :] = jnp.dot(
            left_ref[at : at + strip, :], right, preferred_element_type=F32
        )

    @pl.loop(0, arrived_ref.shape[0])
    def _(source):
        for rank in range(limit):
            row = row_label_ref[source * limit + rank]
            for slot in range(slots):
                col = col_label_ref[(source * limit + rank) * slots + slot] - step * per_chunk

                @pl.when((row >= 0) & (col >= 0) & (col < per_chunk))
                def _():
                    down = pl.ds(pl.multiple_of(row * tile, tile), tile)
                    along = pl.ds(pl.multiple_of(col * tile, tile), tile)
                    trailing_ref[down, along] += (
                        arrived_ref[source, slot, rank * tile : (rank + 1) * tile, :]
                        .astype(I32)
                        .astype(F32)
                        * scales_ref[source, rank : rank + 1, slot * tile : (slot + 1) * tile]
                    )

    unit = lax.broadcasted_iota(I32, (tile, tile), 0) == lax.broadcasted_iota(
        I32, (tile, tile), 1
    )
    for col in range(per_chunk):
        row = first_col + step * per_chunk + col - scen * rows_own

        @pl.when((row >= 0) & (row < rows_own))
        def _():
            down = pl.ds(pl.multiple_of(row * tile, tile), tile)
            trailing_ref[down, col * tile : (col + 1) * tile] += jnp.where(
                unit, diag_ref[pl.ds(row, 1), :], 0.0
            )


def finish(place, row_labels, col_labels, lead_labels, arrays, limit, width):
    lower, diag = arrays[5], arrays[7]
    tile = lower.shape[0]
    rows = diag.shape[0] * tile
    chunk = min(512, width)
    return pl.pallas_call(
        lambda *refs: finish_kernel(limit, *refs),
        grid_spec=pltpu.PrefetchScalarGridSpec(
            num_scalar_prefetch=4,
            grid=(width // chunk,),
            in_specs=[VMEM] * len(arrays),
            out_specs=[
                pl.BlockSpec((rows, tile), lambda c, *_: (0, 0)),
                pl.BlockSpec((rows, chunk), lambda c, *_: (0, c)),
            ],
            scratch_shapes=[pltpu.VMEM((rows, 3 * tile), BF16), pltpu.VMEM((tile, width), F32)],
        ),
        out_shape=(
            jax.ShapeDtypeStruct((rows, tile), F32),
            jax.ShapeDtypeStruct((rows, width), F32),
        ),
        name="finish",
        compiler_params=pltpu.CompilerParams(vmem_limit_bytes=48 * MIB),
    )(place, row_labels, col_labels, lead_labels, *arrays)


def per_device(factor_inv, coupling, first_diag, pattern):
    rows_own, tile = first_diag.shape
    scen_count = lax.axis_size("scen")
    link_count = lax.axis_size("link")
    scen_pos = lax.axis_index("scen")
    link_pos = lax.axis_index("link")
    per_link = rows_own * scen_count // link_count
    scen_here, spread = pattern.shape
    width = coupling.shape[2]
    slots = width // tile

    own = jnp.einsum("snm,smc->snc", factor_inv, coupling, preferred_element_type=F32).astype(BF16)
    gathered = lax.all_gather(own, "link", axis=0, tiled=False)

    share = lax.dot_general(
        own[0, :, :tile], own[0, :, :tile], (((0,), (0,)), ((), ())), preferred_element_type=F32
    )
    unit = jnp.eye(tile, dtype=F32)
    share = share + jnp.where(scen_pos == 0, first_diag[0][:, None] * unit, 0.0)
    padded = jnp.pad(pattern, ((0, 8 - scen_here), (0, 128 - spread)))
    corner, patterns = sum_corner(share, padded, scen_count, link_count)
    patterns = patterns[:, :scen_here, :spread]
    lower, inverse = lead_factor(corner)

    picks = scen_here * slots
    owners_here = max(1, per_link // rows_own)
    limit = max(1, (picks + owners_here - 1) // owners_here)
    listed = jnp.arange(scen_here * spread, dtype=I32)

    def targets(blocks):
        owners = blocks // rows_own
        earlier = (owners[..., :, None] == owners[..., None, :]) & (
            listed[None, :] < listed[:, None]
        )
        return owners * limit + jnp.sum(earlier.astype(I32), axis=-1)

    coded, scales = contribute(
        targets(pattern.reshape(-1)), gathered, own, tile, scen_count, limit
    )

    blocks = patterns.reshape(scen_count, scen_here * spread)
    places = scen_pos * limit + jnp.arange(limit, dtype=I32)
    hit = targets(blocks)[:, :, None] == places[None, None, :]
    row_labels = (
        jnp.sum(jnp.where(hit, blocks[:, :, None] - scen_pos * rows_own + 1, 0), axis=1) - 1
    )
    own_cols = (
        lax.dynamic_slice_in_dim(patterns, link_pos * slots, slots, 2) - link_pos * per_link
    )
    slab_cols = jnp.repeat(own_cols, spread, axis=1)
    col_labels = jnp.sum(jnp.where(hit[:, :, :, None], slab_cols[:, :, None, :], 0), axis=1)
    lead_labels = own_cols[:, 0, :]
    first_col = (col_labels[:, :, 0] == 0).reshape(-1)
    row_labels = row_labels.reshape(-1)
    weight = (
        (row_labels[None, :] == jnp.arange(rows_own, dtype=I32)[:, None]) & first_col[None, :]
    ).astype(F32)

    arrived, arrived_scales, lead, lead_scales, column = exchange(
        weight, coded, scales, tile, limit, link_count
    )
    place = jnp.stack([scen_pos, link_pos]).astype(I32)
    arrays = (
        arrived, arrived_scales, lead, lead_scales, column, lower, inverse, first_diag,
    )
    return finish(
        place, row_labels, col_labels.reshape(-1), lead_labels.reshape(-1), arrays, limit,
        per_link * tile,
    )


def solution(mesh):
    in_specs = (P("scen", None, None), P("scen", None, "link"), P("scen", None), P("scen", None))
    out_specs = (P("scen", None), P("scen", "link"))
    return jax.shard_map(
        per_device, mesh=mesh, in_specs=in_specs, out_specs=out_specs, check_vma=False
    )
```

```python
import jax
import jax.numpy as jnp
from jax import lax
from jax.experimental import pallas as pl
from jax.experimental.pallas import tpu as pltpu
from jax.sharding import PartitionSpec as P

F32 = jnp.float32
BF16 = jnp.bfloat16
I32 = jnp.int32
I16 = jnp.int16
HIGHEST = lax.Precision.HIGHEST
MESH = pl.DeviceIdType.MESH
VMEM = pl.BlockSpec(memory_space=pltpu.VMEM)
SMEM = pl.BlockSpec(memory_space=pltpu.SMEM)
MIB = 2**20
LEVELS = 32767.0


def factor(work):
    size = work.shape[0]
    inverse = (
        lax.broadcasted_iota(I32, (size, size), 0) == lax.broadcasted_iota(I32, (size, size), 1)
    ).astype(F32)
    upper_rows, inverse_rows = [], []
    base = 0
    for j in range(size):
        start = j // 8 * 8
        if start > base:
            work, inverse, base = work[start - base :], inverse[start - base :], start
        k = j - base
        column = work[:, j : j + 1]
        pivot = column[k : k + 1]
        row, inverse_row = work[k : k + 1], inverse[k : k + 1]
        scale = 1.0 / jnp.sqrt(pivot)
        upper_rows.append(row * scale)
        inverse_rows.append(inverse_row * scale)
        if j + 1 < size:
            below = lax.broadcasted_iota(I32, (size - base, 1), 0) > k
            ratio = jnp.where(below, column * (1.0 / pivot), 0.0)
            work = work - ratio * row
            inverse = inverse - ratio * inverse_row
    return jnp.concatenate(upper_rows, axis=0), jnp.concatenate(inverse_rows, axis=0)


def factor_into(corner_ref, lower_ref, inverse_ref):
    upper, inverse = factor(corner_ref[...])
    size = upper.shape[0]
    keep = lax.broadcasted_iota(I32, (size, size), 0) <= lax.broadcasted_iota(
        I32, (size, size), 1
    )
    lower_ref[...] = jnp.where(keep, upper, 0.0).T
    inverse_ref[...] = inverse


def greet(scen_count, link_count):
    scen, link = lax.axis_index("scen"), lax.axis_index("link")
    barrier = pltpu.get_barrier_semaphore()

    @pl.loop(1, scen_count)
    def _(step):
        pl.semaphore_signal(
            barrier,
            inc=1,
            device_id={"scen": lax.rem(scen + step, scen_count)},
            device_id_type=MESH,
        )

    for step in range(1, link_count):
        pl.semaphore_signal(
            barrier,
            inc=1,
            device_id={"link": lax.rem(link + step, link_count)},
            device_id_type=MESH,
        )
    pl.semaphore_wait(barrier, scen_count + link_count - 2)


def gather_kernel(
    scen_count,
    link_count,
    factor_ref,
    coupling_ref,
    diag_ref,
    pattern_ref,
    gathered_ref,
    corner_ref,
    patterns_ref,
    held_ref,
    shares_ref,
    held_sem,
    scen_send,
    scen_recv,
    slab_send,
    slab_recv,
    link_send,
    link_recv,
):
    scen, link = lax.axis_index("scen"), lax.axis_index("link")
    scen_here, depth, width = coupling_ref.shape
    tile = corner_ref.shape[0]
    halves = 2
    rows = depth // halves
    half = link_count // 2
    twin = link + 1 - 2 * lax.rem(link, 2)
    across = lax.rem(link + half, link_count)

    def fetch(scenario):
        return pltpu.make_async_copy(
            factor_ref.at[scenario], held_ref.at[scenario], held_sem.at[scenario]
        )

    for scenario in range(scen_here):
        fetch(scenario).start()
    greet(scen_count, link_count)

    def share_copy(source, peer):
        return pltpu.make_async_remote_copy(
            src_ref=shares_ref.at[scen],
            dst_ref=shares_ref.at[source],
            send_sem=scen_send.at[0, peer],
            recv_sem=scen_recv.at[0, source],
            device_id={"scen": peer},
            device_id_type=MESH,
        )

    def pattern_copy(source, peer):
        return pltpu.make_async_remote_copy(
            src_ref=pattern_ref,
            dst_ref=patterns_ref.at[source],
            send_sem=scen_send.at[1, peer],
            recv_sem=scen_recv.at[1, source],
            device_id={"scen": peer},
            device_id_type=MESH,
        )

    def corner_copy(target):
        return pltpu.make_async_remote_copy(
            src_ref=corner_ref,
            dst_ref=corner_ref,
            send_sem=link_send.at[target],
            recv_sem=link_recv,
            device_id={"link": target},
            device_id_type=MESH,
        )

    def slab_copy(way, scenario, piece, source, target):
        at = gathered_ref.at[source, scenario, pl.ds(piece * rows, rows)]
        return pltpu.make_async_remote_copy(
            src_ref=at,
            dst_ref=at,
            send_sem=slab_send.at[way, scenario, piece],
            recv_sem=slab_recv.at[way, scenario, piece],
            device_id={"link": target},
            device_id_type=MESH,
        )

    def over_peers(act):
        @pl.loop(1, scen_count)
        def _(step):
            act(lax.rem(scen + step, scen_count))

    for scenario in range(scen_here):
        fetch(scenario).wait()
        for piece in range(halves):
            strip = rows // 2
            for part in range(2):
                down = slice(piece * rows + part * strip, piece * rows + (part + 1) * strip)
                gathered_ref[link, scenario, down, :] = jnp.dot(
                    held_ref[scenario, down, :],
                    coupling_ref[scenario],
                    preferred_element_type=F32,
                ).astype(BF16)
            slab_copy(1, scenario, piece, link, across).start()
            slab_copy(0, scenario, piece, link, twin).start()
        if scenario == 0:

            @pl.when(link == 0)
            def _():
                lead = gathered_ref[0, 0, :, :tile]
                share = lax.dot_general(
                    lead, lead, (((0,), (0,)), ((), ())), preferred_element_type=F32
                )
                unit = lax.broadcasted_iota(I32, (tile, tile), 0) == lax.broadcasted_iota(
                    I32, (tile, tile), 1
                )
                shares_ref[scen] = share + jnp.where(unit & (scen == 0), diag_ref[0:1, :], 0.0)
                over_peers(lambda peer: share_copy(scen, peer).start())

    patterns_ref[scen] = pattern_ref[...]
    over_peers(lambda peer: pattern_copy(scen, peer).start())

    @pl.when(link == 0)
    def _():
        over_peers(lambda peer: share_copy(peer, peer).wait_recv())
        corner_ref[...] = shares_ref[0]

        @pl.loop(1, scen_count)
        def _(source):
            corner_ref[...] += shares_ref[source]

        for target in range(1, link_count):
            corner_copy(target).start()

    pieces = [(scenario, piece) for scenario in range(scen_here) for piece in range(halves)]
    for scenario, piece in pieces:
        slab_copy(1, scenario, piece, across, across).wait_recv()
        slab_copy(2, scenario, piece, across, twin).start()
    beyond = lax.rem(twin + half, link_count)
    for scenario, piece in pieces:
        slab_copy(0, scenario, piece, twin, twin).wait_recv()
        slab_copy(2, scenario, piece, beyond, twin).wait_recv()
    for scenario, piece in pieces:
        slab_copy(0, scenario, piece, link, twin).wait_send()
        slab_copy(1, scenario, piece, link, across).wait_send()
        slab_copy(2, scenario, piece, across, twin).wait_send()

    @pl.when(link == 0)
    def _():
        over_peers(lambda peer: share_copy(scen, peer).wait_send())
        for target in range(1, link_count):
            corner_copy(target).wait_send()

    def finish_pattern(peer):
        pattern_copy(scen, peer).wait_send()
        pattern_copy(peer, peer).wait_recv()

    over_peers(finish_pattern)

    @pl.when(link != 0)
    def _():
        corner_copy(0).wait_recv()


def gather(factor_inv, coupling, diag, pattern, scen_count, link_count):
    tile = diag.shape[1]
    dma = pltpu.SemaphoreType.DMA
    pieces = (3, coupling.shape[0], 2)
    return pl.pallas_call(
        lambda *refs: gather_kernel(scen_count, link_count, *refs),
        out_shape=(
            jax.ShapeDtypeStruct((link_count,) + coupling.shape, BF16),
            jax.ShapeDtypeStruct((tile, tile), F32),
            jax.ShapeDtypeStruct((scen_count,) + pattern.shape, I32),
        ),
        in_specs=[pl.BlockSpec(memory_space=pl.ANY), VMEM, VMEM, VMEM],
        out_specs=(VMEM, VMEM, VMEM),
        scratch_shapes=[
            pltpu.VMEM(factor_inv.shape, BF16),
            pltpu.VMEM((scen_count, tile, tile), F32),
            dma((coupling.shape[0],)),
            dma((2, scen_count)),
            dma((2, scen_count)),
            dma(pieces),
            dma(pieces),
            dma((link_count,)),
            dma,
        ],
        name="gather",
        compiler_params=pltpu.CompilerParams(
            collective_id=0, has_side_effects=True, vmem_limit_bytes=40 * MIB
        ),
    )(factor_inv, coupling, diag, pattern)


def contribute_kernel(limit, clear, target_ref, link_ref, rows_ref, own_ref, coded_ref, scales_ref):
    scenario, piece = pl.program_id(0), pl.program_id(1)
    tile = coded_ref.shape[3]
    slots = coded_ref.shape[1]
    spread = slots * pl.num_programs(1)
    if clear:

        @pl.when((scenario == 0) & (piece == 0))
        def _():
            coded_ref[...] = jnp.zeros_like(coded_ref)
            scales_ref[...] = jnp.zeros_like(scales_ref)

    product = lax.dot_general(
        rows_ref[0, 0], own_ref[0, 0], (((0,), (0,)), ((), ())), preferred_element_type=F32
    )
    for slab in range(slots):
        values = product[slab * tile : (slab + 1) * tile]
        target = target_ref[scenario * spread + piece * slots + slab]
        dest = target // limit
        rank = target - dest * limit
        peak = jnp.max(jnp.abs(values), axis=0, keepdims=True)
        gain = jnp.where(peak > 1e-30, LEVELS / jnp.maximum(peak, 1e-30), 0.0)
        code = jnp.round(values * gain).astype(I32).astype(I16)
        scales_ref[dest, pl.ds(rank, 1), :] = peak * (1.0 / LEVELS)
        for slot in range(slots):
            coded_ref[dest, slot, pl.ds(pl.multiple_of(rank * tile, tile), tile), :] = code[
                :, slot * tile : (slot + 1) * tile
            ]


def contribute(target, link, gathered, tile, scen_count, limit):
    link_count, scen_here, depth, width = gathered.shape
    slots = width // tile
    clear = scen_count * limit > target.shape[0]
    return pl.pallas_call(
        lambda *refs: contribute_kernel(limit, clear, *refs),
        grid_spec=pltpu.PrefetchScalarGridSpec(
            num_scalar_prefetch=2,
            grid=(scen_here, link_count),
            in_specs=[
                pl.BlockSpec((1, 1, depth, width), lambda i, j, *_: (j, i, 0, 0)),
                pl.BlockSpec((1, 1, depth, width), lambda i, j, _, link: (link[0], i, 0, 0)),
            ],
            out_specs=[
                pl.BlockSpec((scen_count, slots, limit * tile, tile), lambda i, j, *_: (0, 0, 0, 0)),
                pl.BlockSpec((scen_count, 8, width), lambda i, j, *_: (0, 0, 0)),
            ],
        ),
        out_shape=(
            jax.ShapeDtypeStruct((scen_count, slots, limit * tile, tile), I16),
            jax.ShapeDtypeStruct((scen_count, 8, width), F32),
        ),
        name="contribute",
        compiler_params=pltpu.CompilerParams(vmem_limit_bytes=40 * MIB),
    )(target, link, gathered, gathered)


def exchange_kernel(
    scen_count,
    link_count,
    limit,
    weight_ref,
    coded_ref,
    scales_ref,
    corner_ref,
    arrived_ref,
    arrived_scales_ref,
    lead_ref,
    lead_scales_ref,
    column_ref,
    lower_ref,
    inverse_ref,
    wide_ref,
    send_sem,
    recv_sem,
    local_sem,
    lead_send,
    lead_recv,
    link_send,
    link_recv,
):
    scen, link = lax.axis_index("scen"), lax.axis_index("link")
    tile = coded_ref.shape[3]
    slots = coded_ref.shape[1]
    rows_own = column_ref.shape[0] // tile
    chunks = link_recv.shape[0]
    greet(scen_count, link_count)

    def ends(kind, source, dest):
        if kind == 0:
            return scales_ref.at[dest], arrived_scales_ref.at[source]
        return coded_ref.at[dest, kind - 1], arrived_ref.at[source, kind - 1]

    def copy(kind, source, peer):
        src, dst = ends(kind, source, peer)
        return pltpu.make_async_remote_copy(
            src_ref=src,
            dst_ref=dst,
            send_sem=send_sem.at[kind, peer],
            recv_sem=recv_sem.at[kind, source],
            device_id={"scen": peer},
            device_id_type=MESH,
        )

    def keep(kind):
        src, dst = ends(kind, scen, scen)
        return pltpu.make_async_copy(src, dst, local_sem.at[kind])

    def over_peers(act):
        @pl.loop(1, scen_count)
        def _(step):
            act(lax.rem(scen + step, scen_count))

    first, later = (0, 1), tuple(range(2, slots + 1))

    def start_first(peer):
        for kind in first:
            copy(kind, scen, peer).start()

    def start_later(peer):
        for kind in later:
            copy(kind, scen, peer).start()

    def finish_send(kinds):
        def act(peer):
            for kind in kinds:
                copy(kind, scen, peer).wait_send()

        return act

    def finish_recv(kinds):
        def act(peer):
            for kind in kinds:
                copy(kind, peer, peer).wait_recv()

        return act

    line = scen_count // 2
    spot, side = scen // 2, lax.rem(scen, 2)
    pair = scen + 1 - 2 * side

    def lead_copies(way, block, target):
        return [
            pltpu.make_async_remote_copy(
                src_ref=ref.at[block],
                dst_ref=ref.at[block],
                send_sem=lead_send.at[which, way, block],
                recv_sem=lead_recv.at[which, block],
                device_id={"scen": target},
                device_id_type=MESH,
            )
            for which, ref in enumerate((lead_ref, lead_scales_ref))
        ]

    def lead_wait(block):
        for one in lead_copies(2, block, pair):
            one.wait_recv()

    def lead_pass(block, left, right, act):
        @pl.when(left & (spot > 0))
        def _():
            for one in lead_copies(0, block, lax.rem(scen + scen_count - 2, scen_count)):
                act(one)

        @pl.when(right & (spot < line - 1))
        def _():
            for one in lead_copies(1, block, lax.rem(scen + 2, scen_count)):
                act(one)

        for one in lead_copies(2, block, pair):
            act(one)

    def begin(one):
        one.start()

    def end(one):
        one.wait_send()

    def over_line(act, arriving):
        @pl.loop(1, line)
        def _(step):
            @pl.when(spot - step >= 0)
            def _():
                block = scen - 2 * step
                if arriving:
                    lead_wait(block)
                lead_pass(block, False, True, act)

            @pl.when(spot + step < line)
            def _():
                block = scen + 2 * step
                if arriving:
                    lead_wait(block)
                lead_pass(block, True, False, act)

    over_peers(start_first)
    lead_ref[scen] = coded_ref[0, :, :tile, :]
    lead_scales_ref[scen] = scales_ref[0]
    lead_pass(scen, True, True, begin)
    for kind in first + later:
        keep(kind).start()
    factor_into(corner_ref, lower_ref, inverse_ref)
    over_peers(finish_send(first))
    over_peers(start_later)
    for kind in first + later:
        keep(kind).wait()

    rows = column_ref.shape[0] // chunks

    def column_copy(piece, target, kind):
        at = pl.ds(piece * rows, rows)
        return pltpu.make_async_remote_copy(
            src_ref=column_ref.at[at],
            dst_ref=column_ref.at[at],
            send_sem=link_send.at[kind, piece],
            recv_sem=link_recv.at[piece],
            device_id={"link": target},
            device_id_type=MESH,
        )

    half = link_count // 2

    @pl.when(link == 0)
    def _():
        over_peers(finish_recv(first))

        @pl.loop(0, scen_count)
        def _(source):
            for rank in range(limit):
                at = slice(rank * tile, (rank + 1) * tile)
                wide_ref[source * limit + rank] = (
                    arrived_ref[source, 0, at, :].astype(I32).astype(F32)
                    * arrived_scales_ref[source, rank : rank + 1, :tile]
                )

        per_chunk = rows_own // chunks
        for piece in range(chunks):
            for inner in range(per_chunk):
                block = piece * per_chunk + inner

                def add(listed, total, block=block):
                    return total + weight_ref[block, listed] * wide_ref[listed]

                column_ref[block * tile : (block + 1) * tile, :] = lax.fori_loop(
                    0, scen_count * limit, add, jnp.zeros((tile, tile), F32), unroll=4
                )
            column_copy(piece, half, 0).start()
            for target in range(1, half):
                column_copy(piece, target, target).start()
    over_line(begin, True)

    @pl.when(link == 0)
    def _():
        for piece in range(chunks):
            for kind in range(half):
                column_copy(piece, half, kind).wait_send()

    @pl.when(link != 0)
    def _():
        over_peers(finish_recv(first))
        for piece in range(chunks):
            column_copy(piece, 0, 0).wait_recv()

            @pl.when(link == half)
            def _():
                for target in range(half + 1, link_count):
                    column_copy(piece, target, target - half).start()

        @pl.when(link == half)
        def _():
            for piece in range(chunks):
                for kind in range(1, half):
                    column_copy(piece, half + 1, kind).wait_send()

    @pl.loop(0, line)
    def _(step):
        lead_wait(2 * step + 1 - side)

    lead_pass(scen, True, True, end)
    over_line(end, False)
    over_peers(finish_recv(later))
    over_peers(finish_send(later))


def exchange(weight, coded, scales, corner, limit, link_count):
    tile = corner.shape[0]
    scen_count, slots = coded.shape[:2]
    rows_own = weight.shape[0]
    kinds = slots + 1
    chunks = min(4, rows_own)
    dma = pltpu.SemaphoreType.DMA
    return pl.pallas_call(
        lambda *refs: exchange_kernel(scen_count, link_count, limit, *refs),
        out_shape=(
            jax.ShapeDtypeStruct(coded.shape, I16),
            jax.ShapeDtypeStruct(scales.shape, F32),
            jax.ShapeDtypeStruct((scen_count, slots, tile, tile), I16),
            jax.ShapeDtypeStruct(scales.shape, F32),
            jax.ShapeDtypeStruct((rows_own * tile, tile), F32),
            jax.ShapeDtypeStruct((tile, tile), F32),
            jax.ShapeDtypeStruct((tile, tile), F32),
        ),
        in_specs=[SMEM, VMEM, VMEM, VMEM],
        out_specs=(VMEM,) * 7,
        scratch_shapes=[
            pltpu.VMEM((scen_count * limit, tile, tile), F32),
            dma((kinds, scen_count)),
            dma((kinds, scen_count)),
            dma((kinds,)),
            dma((2, 3, scen_count)),
            dma((2, scen_count)),
            dma((max(1, link_count // 2), chunks)),
            dma((chunks,)),
        ],
        name="exchange",
        compiler_params=pltpu.CompilerParams(
            collective_id=1, has_side_effects=True, vmem_limit_bytes=48 * MIB
        ),
    )(weight, coded, scales, corner)


def split(value):
    high = value.astype(BF16)
    return high, (value - high.astype(F32)).astype(BF16)


def finish_kernel(
    limit,
    place_ref,
    row_label_ref,
    col_label_ref,
    lead_label_ref,
    arrived_ref,
    scales_ref,
    lead_ref,
    lead_scales_ref,
    column_ref,
    lower_ref,
    inverse_ref,
    diag_ref,
    panel_ref,
    trailing_ref,
    left_ref,
    raw_ref,
    list_ref,
    count_ref,
):
    tile = lower_ref.shape[0]
    chunk = trailing_ref.shape[1]
    slots = arrived_ref.shape[1]
    rows_own = diag_ref.shape[0]
    step = pl.program_id(0)
    per_chunk = chunk // tile
    scen, link = place_ref[0], place_ref[1]
    first_col = link * per_chunk * pl.num_programs(0)

    @pl.when(step == 0)
    def _():
        raw_ref[...] = jnp.zeros_like(raw_ref)

        @pl.loop(0, lead_ref.shape[0])
        def _(source):
            for slot in range(slots):
                at = pl.multiple_of(lead_label_ref[source * slots + slot] * tile, tile)
                raw_ref[:, pl.ds(at, tile)] += (
                    lead_ref[source, slot].astype(I32).astype(F32)
                    * lead_scales_ref[source, 0:1, slot * tile : (slot + 1) * tile]
                )

        group = min(4, rows_own) * tile
        for start in range(0, rows_own * tile, group):
            at = slice(start, start + group)
            solved = lax.dot_general(
                column_ref[at, :],
                inverse_ref[...],
                (((1,), (1,)), ((), ())),
                precision=HIGHEST,
                preferred_element_type=F32,
            )
            if start == 0:
                top = jnp.where(scen == 0, lower_ref[...], solved[:tile])
                solved = jnp.concatenate([top, solved[tile:]], axis=0)
            panel_ref[at, :] = solved
            high, low = split(-solved)
            left_ref[at, :tile] = high
            left_ref[at, tile : 2 * tile] = low
            left_ref[at, 2 * tile :] = high

        for other in range(count_ref.shape[0]):
            count_ref[other] = 0

        @pl.loop(0, list_ref.shape[1])
        def _(entry):
            @pl.when(row_label_ref[entry // slots] >= 0)
            def _():
                owner = col_label_ref[entry] // per_chunk
                held = count_ref[owner]
                list_ref[owner, held] = entry
                count_ref[owner] = held + 1

    part = jnp.dot(
        inverse_ref[...],
        raw_ref[:, pl.ds(pl.multiple_of(step * chunk, chunk), chunk)],
        precision=HIGHEST,
        preferred_element_type=F32,
    )
    is_lead = (link == 0) & (step == 0)
    top = jnp.where(is_lead, lower_ref[...].T, part[:, :tile])
    part = jnp.concatenate([top, part[:, tile:]], axis=1) if per_chunk > 1 else top
    high, low = split(part)
    right = jnp.concatenate([high, high, low], axis=0)
    strip = 2 * tile if rows_own % 2 == 0 else tile
    for at in range(0, rows_own * tile, strip):
        trailing_ref[at : at + strip, :] = jnp.dot(
            left_ref[at : at + strip, :], right, preferred_element_type=F32
        )

    @pl.loop(0, count_ref[step])
    def _(place):
        entry = list_ref[step, place]
        listed = entry // slots
        slot = entry - listed * slots
        source = listed // limit
        rank = listed - source * limit
        col = col_label_ref[entry] - step * per_chunk
        down = pl.ds(pl.multiple_of(row_label_ref[listed] * tile, tile), tile)
        along = pl.ds(pl.multiple_of(col * tile, tile), tile)
        from_rows = pl.ds(pl.multiple_of(rank * tile, tile), tile)
        from_lanes = pl.ds(pl.multiple_of(slot * tile, tile), tile)
        scales = scales_ref[source, :, from_lanes]
        picked = lax.broadcasted_iota(I32, scales.shape, 0) == rank
        scale = jnp.sum(jnp.where(picked, scales, 0.0), axis=0, keepdims=True)
        codes = arrived_ref[source, slot, from_rows, :]
        trailing_ref[down, along] += codes.astype(I32).astype(F32) * scale

    unit = lax.broadcasted_iota(I32, (tile, tile), 0) == lax.broadcasted_iota(
        I32, (tile, tile), 1
    )
    for col in range(per_chunk):
        row = first_col + step * per_chunk + col - scen * rows_own

        @pl.when((row >= 0) & (row < rows_own))
        def _():
            down = pl.ds(pl.multiple_of(row * tile, tile), tile)
            trailing_ref[down, col * tile : (col + 1) * tile] += jnp.where(
                unit, diag_ref[pl.ds(row, 1), :], 0.0
            )


def finish(place, row_labels, col_labels, lead_labels, arrays, limit, width):
    lower, diag = arrays[5], arrays[7]
    tile = lower.shape[0]
    rows = diag.shape[0] * tile
    chunk = min(512, width)
    return pl.pallas_call(
        lambda *refs: finish_kernel(limit, *refs),
        grid_spec=pltpu.PrefetchScalarGridSpec(
            num_scalar_prefetch=4,
            grid=(width // chunk,),
            in_specs=[VMEM] * len(arrays),
            out_specs=[
                pl.BlockSpec((rows, tile), lambda c, *_: (0, 0)),
                pl.BlockSpec((rows, chunk), lambda c, *_: (0, c)),
            ],
            scratch_shapes=[
                pltpu.VMEM((rows, 3 * tile), BF16),
                pltpu.VMEM((tile, width), F32),
                pltpu.SMEM((width // chunk, col_labels.shape[0]), I32),
                pltpu.SMEM((width // chunk,), I32),
            ],
        ),
        out_shape=(
            jax.ShapeDtypeStruct((rows, tile), F32),
            jax.ShapeDtypeStruct((rows, width), F32),
        ),
        name="finish",
        compiler_params=pltpu.CompilerParams(vmem_limit_bytes=48 * MIB),
    )(place, row_labels, col_labels, lead_labels, *arrays)


def per_device(factor_inv, coupling, first_diag, pattern):
    rows_own, tile = first_diag.shape
    scen_count = lax.axis_size("scen")
    link_count = lax.axis_size("link")
    scen_pos = lax.axis_index("scen")
    link_pos = lax.axis_index("link")
    per_link = rows_own * scen_count // link_count
    scen_here, spread = pattern.shape
    width = coupling.shape[2]
    slots = width // tile

    padded = jnp.pad(pattern, ((0, 8 - scen_here), (0, 128 - spread)))
    gathered, corner, patterns = gather(
        factor_inv, coupling, first_diag, padded, scen_count, link_count
    )
    patterns = patterns[:, :scen_here, :spread]

    picks = scen_here * slots
    owners_here = max(1, per_link // rows_own)
    limit = max(1, (picks + owners_here - 1) // owners_here)
    listed = jnp.arange(scen_here * spread, dtype=I32)

    def targets(blocks):
        owners = blocks // rows_own
        earlier = (owners[..., :, None] == owners[..., None, :]) & (
            listed[None, :] < listed[:, None]
        )
        return owners * limit + jnp.sum(earlier.astype(I32), axis=-1)

    coded, scales = contribute(
        targets(pattern.reshape(-1)), link_pos[None].astype(I32), gathered, tile, scen_count, limit
    )

    blocks = patterns.reshape(scen_count, scen_here * spread)
    places = scen_pos * limit + jnp.arange(limit, dtype=I32)
    hit = targets(blocks)[:, :, None] == places[None, None, :]
    row_labels = (
        jnp.sum(jnp.where(hit, blocks[:, :, None] - scen_pos * rows_own + 1, 0), axis=1) - 1
    )
    own_cols = (
        lax.dynamic_slice_in_dim(patterns, link_pos * slots, slots, 2) - link_pos * per_link
    )
    slab_cols = jnp.repeat(own_cols, spread, axis=1)
    col_labels = jnp.sum(jnp.where(hit[:, :, :, None], slab_cols[:, :, None, :], 0), axis=1)
    lead_labels = own_cols[:, 0, :]
    first_col = (col_labels[:, :, 0] == 0).reshape(-1)
    row_labels = row_labels.reshape(-1)
    weight = (
        (row_labels[None, :] == jnp.arange(rows_own, dtype=I32)[:, None]) & first_col[None, :]
    ).astype(F32)

    arrived, arrived_scales, lead, lead_scales, column, lower, inverse = exchange(
        weight, coded, scales, corner, limit, link_count
    )
    place = jnp.stack([scen_pos, link_pos]).astype(I32)
    arrays = (
        arrived, arrived_scales, lead, lead_scales, column, lower, inverse, first_diag,
    )
    return finish(
        place, row_labels, col_labels.reshape(-1), lead_labels.reshape(-1), arrays, limit,
        per_link * tile,
    )


def solution(mesh):
    in_specs = (P("scen", None, None), P("scen", None, "link"), P("scen", None), P("scen", None))
    out_specs = (P("scen", None), P("scen", "link"))
    return jax.shard_map(
        per_device, mesh=mesh, in_specs=in_specs, out_specs=out_specs, check_vma=False
    )
```

```python
import jax
import jax.numpy as jnp
from jax import lax
from jax.experimental import pallas as pl
from jax.experimental.pallas import tpu as pltpu
from jax.sharding import PartitionSpec as P

F32 = jnp.float32
BF16 = jnp.bfloat16
I32 = jnp.int32
I16 = jnp.int16
HIGHEST = lax.Precision.HIGHEST
MESH = pl.DeviceIdType.MESH
VMEM = pl.BlockSpec(memory_space=pltpu.VMEM)
ANY = pl.BlockSpec(memory_space=pl.ANY)
MIB = 2**20
LEVELS = 32767.0


def factor(work):
    size = work.shape[0]
    inverse = (
        lax.broadcasted_iota(I32, (size, size), 0) == lax.broadcasted_iota(I32, (size, size), 1)
    ).astype(F32)
    upper_rows, inverse_rows = [], []
    base = 0
    for j in range(size):
        start = j // 8 * 8
        if start > base:
            work, inverse, base = work[start - base :], inverse[start - base :], start
        k = j - base
        column = work[:, j : j + 1]
        pivot = column[k : k + 1]
        row, inverse_row = work[k : k + 1], inverse[k : k + 1]
        scale = 1.0 / jnp.sqrt(pivot)
        upper_rows.append(row * scale)
        inverse_rows.append(inverse_row * scale)
        if j + 1 < size:
            below = lax.broadcasted_iota(I32, (size - base, 1), 0) > k
            ratio = jnp.where(below, column * (1.0 / pivot), 0.0)
            work = work - ratio * row
            inverse = inverse - ratio * inverse_row
    return jnp.concatenate(upper_rows, axis=0), jnp.concatenate(inverse_rows, axis=0)


def factor_into(corner_ref, lower_ref, inverse_ref):
    upper, inverse = factor(corner_ref[...])
    size = upper.shape[0]
    keep = lax.broadcasted_iota(I32, (size, size), 0) <= lax.broadcasted_iota(
        I32, (size, size), 1
    )
    lower_ref[...] = jnp.where(keep, upper, 0.0).T
    inverse_ref[...] = inverse


def greet(scen_count, link_count):
    scen, link = lax.axis_index("scen"), lax.axis_index("link")
    barrier = pltpu.get_barrier_semaphore()

    @pl.loop(1, scen_count)
    def _(step):
        pl.semaphore_signal(
            barrier,
            inc=1,
            device_id={"scen": lax.rem(scen + step, scen_count)},
            device_id_type=MESH,
        )

    for step in range(1, link_count):
        pl.semaphore_signal(
            barrier,
            inc=1,
            device_id={"link": lax.rem(link + step, link_count)},
            device_id_type=MESH,
        )
    pl.semaphore_wait(barrier, scen_count + link_count - 2)


def gather_kernel(
    scen_count,
    link_count,
    factor_ref,
    coupling_ref,
    diag_ref,
    pattern_ref,
    gathered_ref,
    corner_ref,
    patterns_ref,
    held_ref,
    columns_ref,
    first_ref,
    own_ref,
    shares_ref,
    held_sem,
    kept_sem,
    scen_send,
    scen_recv,
    slab_send,
    slab_recv,
    link_send,
    link_recv,
):
    scen, link = lax.axis_index("scen"), lax.axis_index("link")
    scen_here, depth, width = coupling_ref.shape
    tile = corner_ref.shape[0]
    halves = 2
    rows = depth // halves
    half = link_count // 2
    twin = link + 1 - 2 * lax.rem(link, 2)
    across = lax.rem(link + half, link_count)

    def fetch(which, scenario):
        src, dst = ((factor_ref, held_ref), (coupling_ref, columns_ref))[which]
        return pltpu.make_async_copy(
            src.at[scenario], dst.at[scenario], held_sem.at[which, scenario]
        )

    def keep(scenario):
        return pltpu.make_async_copy(
            own_ref.at[scenario], gathered_ref.at[link, scenario], kept_sem.at[scenario]
        )

    first = pltpu.make_async_copy(diag_ref, first_ref, held_sem.at[2, 0])
    for scenario in range(scen_here):
        for which in (1, 0):
            fetch(which, scenario).start()
    first.start()
    greet(scen_count, link_count)

    def share_copy(source, peer):
        return pltpu.make_async_remote_copy(
            src_ref=shares_ref.at[scen],
            dst_ref=shares_ref.at[source],
            send_sem=scen_send.at[0, peer],
            recv_sem=scen_recv.at[0, source],
            device_id={"scen": peer},
            device_id_type=MESH,
        )

    def pattern_copy(source, peer):
        return pltpu.make_async_remote_copy(
            src_ref=pattern_ref,
            dst_ref=patterns_ref.at[source],
            send_sem=scen_send.at[1, peer],
            recv_sem=scen_recv.at[1, source],
            device_id={"scen": peer},
            device_id_type=MESH,
        )

    def corner_copy(target):
        return pltpu.make_async_remote_copy(
            src_ref=corner_ref,
            dst_ref=corner_ref,
            send_sem=link_send.at[target],
            recv_sem=link_recv,
            device_id={"link": target},
            device_id_type=MESH,
        )

    def slab_copy(way, scenario, piece, source, target):
        down = pl.ds(piece * rows, rows)
        at = gathered_ref.at[source, scenario, down]
        return pltpu.make_async_remote_copy(
            src_ref=at if way == 2 else own_ref.at[scenario, down],
            dst_ref=at,
            send_sem=slab_send.at[way, scenario, piece],
            recv_sem=slab_recv.at[way, scenario, piece],
            device_id={"link": target},
            device_id_type=MESH,
        )

    def over_peers(act):
        @pl.loop(1, scen_count)
        def _(step):
            act(lax.rem(scen + step, scen_count))

    for scenario in range(scen_here):
        fetch(1, scenario).wait()
        fetch(0, scenario).wait()
        for piece in range(halves):
            strip = rows // 2
            for part in range(2):
                down = slice(piece * rows + part * strip, piece * rows + (part + 1) * strip)
                own_ref[scenario, down, :] = jnp.dot(
                    held_ref[scenario, down, :],
                    columns_ref[scenario],
                    preferred_element_type=F32,
                ).astype(BF16)
            slab_copy(1, scenario, piece, link, across).start()
            slab_copy(0, scenario, piece, link, twin).start()
        keep(scenario).start()
        if scenario == 0:
            first.wait()

            @pl.when(link == 0)
            def _():
                lead = own_ref[0, :, :tile]
                share = lax.dot_general(
                    lead, lead, (((0,), (0,)), ((), ())), preferred_element_type=F32
                )
                unit = lax.broadcasted_iota(I32, (tile, tile), 0) == lax.broadcasted_iota(
                    I32, (tile, tile), 1
                )
                shares_ref[scen] = share + jnp.where(unit & (scen == 0), first_ref[0:1, :], 0.0)
                over_peers(lambda peer: share_copy(scen, peer).start())

    patterns_ref[scen] = pattern_ref[...]
    over_peers(lambda peer: pattern_copy(scen, peer).start())

    @pl.when(link == 0)
    def _():
        over_peers(lambda peer: share_copy(peer, peer).wait_recv())
        corner_ref[...] = shares_ref[0]

        @pl.loop(1, scen_count)
        def _(source):
            corner_ref[...] += shares_ref[source]

        for target in range(1, link_count):
            corner_copy(target).start()

    pieces = [(scenario, piece) for scenario in range(scen_here) for piece in range(halves)]
    for scenario, piece in pieces:
        slab_copy(1, scenario, piece, across, across).wait_recv()
        slab_copy(2, scenario, piece, across, twin).start()
    beyond = lax.rem(twin + half, link_count)
    for scenario, piece in pieces:
        slab_copy(0, scenario, piece, twin, twin).wait_recv()
        slab_copy(2, scenario, piece, beyond, twin).wait_recv()
    for scenario, piece in pieces:
        slab_copy(0, scenario, piece, link, twin).wait_send()
        slab_copy(1, scenario, piece, link, across).wait_send()
        slab_copy(2, scenario, piece, across, twin).wait_send()

    @pl.when(link == 0)
    def _():
        over_peers(lambda peer: share_copy(scen, peer).wait_send())
        for target in range(1, link_count):
            corner_copy(target).wait_send()

    for scenario in range(scen_here):
        keep(scenario).wait()

    def finish_pattern(peer):
        pattern_copy(scen, peer).wait_send()
        pattern_copy(peer, peer).wait_recv()

    over_peers(finish_pattern)

    @pl.when(link != 0)
    def _():
        corner_copy(0).wait_recv()


def gather(factor_inv, coupling, diag, pattern, scen_count, link_count):
    tile = diag.shape[1]
    dma = pltpu.SemaphoreType.DMA
    pieces = (3, coupling.shape[0], 2)
    return pl.pallas_call(
        lambda *refs: gather_kernel(scen_count, link_count, *refs),
        out_shape=(
            jax.ShapeDtypeStruct((link_count,) + coupling.shape, BF16),
            jax.ShapeDtypeStruct((tile, tile), F32),
            jax.ShapeDtypeStruct((scen_count,) + pattern.shape, I32),
        ),
        in_specs=[ANY, ANY, ANY, VMEM],
        out_specs=(ANY, VMEM, VMEM),
        scratch_shapes=[
            pltpu.VMEM(factor_inv.shape, BF16),
            pltpu.VMEM(coupling.shape, BF16),
            pltpu.VMEM(diag.shape, F32),
            pltpu.VMEM(coupling.shape, BF16),
            pltpu.VMEM((scen_count, tile, tile), F32),
            dma((3, coupling.shape[0])),
            dma((coupling.shape[0],)),
            dma((2, scen_count)),
            dma((2, scen_count)),
            dma(pieces),
            dma(pieces),
            dma((link_count,)),
            dma,
        ],
        name="gather",
        compiler_params=pltpu.CompilerParams(
            collective_id=0, has_side_effects=True, vmem_limit_bytes=60 * MIB
        ),
    )(factor_inv, coupling, diag, pattern)


def contribute_kernel(
    limit,
    rows_own,
    clear,
    block_ref,
    link_ref,
    rows_ref,
    own_ref,
    coded_ref,
    scales_ref,
    target_ref,
    count_ref,
):
    scenario, piece = pl.program_id(0), pl.program_id(1)

    @pl.when((scenario == 0) & (piece == 0))
    def _():
        @pl.loop(0, count_ref.shape[0])
        def _(owner):
            count_ref[owner] = 0

        for listed in range(target_ref.shape[0]):
            owner = block_ref[listed] // rows_own
            rank = count_ref[owner]
            target_ref[listed] = owner * limit + rank
            count_ref[owner] = rank + 1

    tile = coded_ref.shape[3]
    slots = coded_ref.shape[1]
    spread = slots * pl.num_programs(1)
    if clear:

        @pl.when((scenario == 0) & (piece == 0))
        def _():
            coded_ref[...] = jnp.zeros_like(coded_ref)
            scales_ref[...] = jnp.zeros_like(scales_ref)

    product = lax.dot_general(
        rows_ref[0, 0], own_ref[0, 0], (((0,), (0,)), ((), ())), preferred_element_type=F32
    )
    for slab in range(slots):
        values = product[slab * tile : (slab + 1) * tile]
        target = target_ref[scenario * spread + piece * slots + slab]
        dest = target // limit
        rank = target - dest * limit
        peak = jnp.max(jnp.abs(values), axis=0, keepdims=True)
        gain = jnp.where(peak > 1e-30, LEVELS / jnp.maximum(peak, 1e-30), 0.0)
        code = jnp.round(values * gain).astype(I32).astype(I16)
        scales_ref[dest, pl.ds(rank, 1), :] = peak * (1.0 / LEVELS)
        for slot in range(slots):
            coded_ref[dest, slot, pl.ds(pl.multiple_of(rank * tile, tile), tile), :] = code[
                :, slot * tile : (slot + 1) * tile
            ]


def contribute(blocks, link, gathered, tile, scen_count, rows_own, limit):
    link_count, scen_here, depth, width = gathered.shape
    slots = width // tile
    clear = scen_count * limit > blocks.shape[0]
    return pl.pallas_call(
        lambda *refs: contribute_kernel(limit, rows_own, clear, *refs),
        grid_spec=pltpu.PrefetchScalarGridSpec(
            num_scalar_prefetch=2,
            grid=(scen_here, link_count),
            in_specs=[
                pl.BlockSpec((1, 1, depth, width), lambda i, j, *_: (j, i, 0, 0)),
                pl.BlockSpec((1, 1, depth, width), lambda i, j, _, link: (link[0], i, 0, 0)),
            ],
            out_specs=[
                pl.BlockSpec((scen_count, slots, limit * tile, tile), lambda i, j, *_: (0, 0, 0, 0)),
                pl.BlockSpec((scen_count, 8, width), lambda i, j, *_: (0, 0, 0)),
            ],
            scratch_shapes=[
                pltpu.SMEM((blocks.shape[0],), I32),
                pltpu.SMEM((scen_count,), I32),
            ],
        ),
        out_shape=(
            jax.ShapeDtypeStruct((scen_count, slots, limit * tile, tile), I16),
            jax.ShapeDtypeStruct((scen_count, 8, width), F32),
        ),
        name="contribute",
        compiler_params=pltpu.CompilerParams(vmem_limit_bytes=61 * MIB),
    )(blocks, link, gathered, gathered)


def exchange_kernel(
    scen_count,
    link_count,
    coded_ref,
    scales_ref,
    corner_ref,
    arrived_ref,
    arrived_scales_ref,
    lead_ref,
    lead_scales_ref,
    column_ref,
    column_scales_ref,
    lower_ref,
    inverse_ref,
    send_sem,
    recv_sem,
    local_sem,
    lead_send,
    lead_recv,
    link_send,
    link_recv,
):
    scen, link = lax.axis_index("scen"), lax.axis_index("link")
    tile = coded_ref.shape[3]
    slots = coded_ref.shape[1]
    greet(scen_count, link_count)

    def ends(kind, source, dest):
        if kind == 0:
            return scales_ref.at[dest], arrived_scales_ref.at[source]
        return coded_ref.at[dest, kind - 1], arrived_ref.at[source, kind - 1]

    def copy(kind, source, peer):
        src, dst = ends(kind, source, peer)
        return pltpu.make_async_remote_copy(
            src_ref=src,
            dst_ref=dst,
            send_sem=send_sem.at[kind, peer],
            recv_sem=recv_sem.at[kind, source],
            device_id={"scen": peer},
            device_id_type=MESH,
        )

    def keep(kind):
        src, dst = ends(kind, scen, scen)
        return pltpu.make_async_copy(src, dst, local_sem.at[kind])

    def over_peers(act):
        @pl.loop(1, scen_count)
        def _(step):
            act(lax.rem(scen + step, scen_count))

    first, later = (0, 1), tuple(range(2, slots + 1))

    def start_first(peer):
        for kind in first:
            copy(kind, scen, peer).start()

    def start_later(peer):
        for kind in later:
            copy(kind, scen, peer).start()

    def finish_send(kinds):
        def act(peer):
            for kind in kinds:
                copy(kind, scen, peer).wait_send()

        return act

    def finish_recv(kinds):
        def act(peer):
            for kind in kinds:
                copy(kind, peer, peer).wait_recv()

        return act

    line = scen_count // 2
    spot, side = scen // 2, lax.rem(scen, 2)
    pair = scen + 1 - 2 * side

    def lead_copies(way, block, target):
        return [
            pltpu.make_async_remote_copy(
                src_ref=ref.at[block],
                dst_ref=ref.at[block],
                send_sem=lead_send.at[which, way, block],
                recv_sem=lead_recv.at[which, block],
                device_id={"scen": target},
                device_id_type=MESH,
            )
            for which, ref in enumerate((lead_ref, lead_scales_ref))
        ]

    def lead_wait(block):
        for one in lead_copies(2, block, pair):
            one.wait_recv()

    def lead_pass(block, left, right, act):
        @pl.when(left & (spot > 0))
        def _():
            for one in lead_copies(0, block, lax.rem(scen + scen_count - 2, scen_count)):
                act(one)

        @pl.when(right & (spot < line - 1))
        def _():
            for one in lead_copies(1, block, lax.rem(scen + 2, scen_count)):
                act(one)

        for one in lead_copies(2, block, pair):
            act(one)

    def begin(one):
        one.start()

    def end(one):
        one.wait_send()

    def over_line(act, arriving):
        @pl.loop(1, line)
        def _(step):
            @pl.when(spot - step >= 0)
            def _():
                block = scen - 2 * step
                if arriving:
                    lead_wait(block)
                lead_pass(block, False, True, act)

            @pl.when(spot + step < line)
            def _():
                block = scen + 2 * step
                if arriving:
                    lead_wait(block)
                lead_pass(block, True, False, act)

    over_peers(start_first)
    lead_ref[scen] = coded_ref[0, :, :tile, :]
    lead_scales_ref[scen] = scales_ref[0]
    lead_pass(scen, True, True, begin)
    for kind in first + later:
        keep(kind).start()
    factor_into(corner_ref, lower_ref, inverse_ref)
    over_peers(finish_send(first))
    over_peers(start_later)
    for kind in first + later:
        keep(kind).wait()

    half = link_count // 2

    def column_copies(source, target, way, relayed):
        pairs = (
            (column_ref if relayed else arrived_ref.at[:, 0], column_ref),
            (column_scales_ref if relayed else arrived_scales_ref, column_scales_ref),
        )
        return [
            pltpu.make_async_remote_copy(
                src_ref=src.at[source],
                dst_ref=dst.at[source],
                send_sem=link_send.at[which, way, source],
                recv_sem=link_recv.at[which, source],
                device_id={"link": target},
                device_id_type=MESH,
            )
            for which, (src, dst) in enumerate(pairs)
        ]

    def column_out(source):
        for target in (half,) + tuple(range(1, half)):
            for one in column_copies(source, target, target % half, False):
                one.start()

    def column_out_end(source):
        for target in (half,) + tuple(range(1, half)):
            for one in column_copies(source, target, target % half, False):
                one.wait_send()

    @pl.when(link == 0)
    def _():
        column_out(scen)

        @pl.loop(1, scen_count)
        def _(step):
            peer = lax.rem(scen + step, scen_count)
            finish_recv(first)(peer)
            column_out(peer)

    over_line(begin, True)

    @pl.when(link == 0)
    def _():
        column_ref[...] = arrived_ref[:, 0]
        column_scales_ref[...] = arrived_scales_ref[...]

        @pl.loop(0, scen_count)
        def _(source):
            column_out_end(source)

    @pl.when(link != 0)
    def _():
        over_peers(finish_recv(first))

        @pl.loop(0, scen_count)
        def _(step):
            source = lax.rem(scen + step, scen_count)
            for one in column_copies(source, 0, 0, True):
                one.wait_recv()

            @pl.when(link == half)
            def _():
                for target in range(half + 1, link_count):
                    for one in column_copies(source, target, target - half, True):
                        one.start()

        @pl.when(link == half)
        def _():
            @pl.loop(0, scen_count)
            def _(source):
                for target in range(half + 1, link_count):
                    for one in column_copies(source, target, target - half, True):
                        one.wait_send()

    @pl.loop(0, line)
    def _(step):
        lead_wait(2 * step + 1 - side)

    lead_pass(scen, True, True, end)
    over_line(end, False)
    over_peers(finish_recv(later))
    over_peers(finish_send(later))


def exchange(coded, scales, corner, link_count):
    tile = corner.shape[0]
    scen_count, slots, rows = coded.shape[:3]
    kinds = slots + 1
    dma = pltpu.SemaphoreType.DMA
    return pl.pallas_call(
        lambda *refs: exchange_kernel(scen_count, link_count, *refs),
        out_shape=(
            jax.ShapeDtypeStruct(coded.shape, I16),
            jax.ShapeDtypeStruct(scales.shape, F32),
            jax.ShapeDtypeStruct((scen_count, slots, tile, tile), I16),
            jax.ShapeDtypeStruct(scales.shape, F32),
            jax.ShapeDtypeStruct((scen_count, rows, tile), I16),
            jax.ShapeDtypeStruct(scales.shape, F32),
            jax.ShapeDtypeStruct((tile, tile), F32),
            jax.ShapeDtypeStruct((tile, tile), F32),
        ),
        in_specs=[VMEM, VMEM, VMEM],
        out_specs=(VMEM,) * 8,
        scratch_shapes=[
            dma((kinds, scen_count)),
            dma((kinds, scen_count)),
            dma((kinds,)),
            dma((2, 3, scen_count)),
            dma((2, scen_count)),
            dma((2, max(1, link_count // 2), scen_count)),
            dma((2, scen_count)),
        ],
        name="exchange",
        compiler_params=pltpu.CompilerParams(
            collective_id=1, has_side_effects=True, vmem_limit_bytes=48 * MIB
        ),
    )(coded, scales, corner)


def split(value):
    high = value.astype(BF16)
    return high, (value - high.astype(F32)).astype(BF16)


def finish_kernel(
    limit,
    spread,
    place_ref,
    block_ref,
    arrived_ref,
    scales_ref,
    lead_ref,
    lead_scales_ref,
    column_ref,
    column_scales_ref,
    lower_ref,
    inverse_ref,
    diag_ref,
    panel_ref,
    trailing_ref,
    left_ref,
    raw_ref,
    sums_ref,
    list_ref,
    row_ref,
    col_ref,
    count_ref,
):
    tile = lower_ref.shape[0]
    chunk = trailing_ref.shape[1]
    slots = arrived_ref.shape[1]
    rows_own = diag_ref.shape[0]
    step = pl.program_id(0)
    per_chunk = chunk // tile
    listed_count = block_ref.shape[0] // lead_ref.shape[0]
    scen, link = place_ref[0], place_ref[1]
    first_col = link * per_chunk * pl.num_programs(0)

    @pl.when(step == 0)
    def _():
        raw_ref[...] = jnp.zeros_like(raw_ref)

        @pl.loop(0, lead_ref.shape[0])
        def _(source):
            for slot in range(slots):
                block = block_ref[source * listed_count + link * slots + slot] - first_col
                at = pl.multiple_of(block * tile, tile)
                raw_ref[:, pl.ds(at, tile)] += (
                    lead_ref[source, slot].astype(I32).astype(F32)
                    * lead_scales_ref[source, 0:1, slot * tile : (slot + 1) * tile]
                )

        sums_ref[...] = jnp.zeros_like(sums_ref)
        for other in range(count_ref.shape[0]):
            count_ref[other] = 0

        @pl.loop(0, lead_ref.shape[0])
        def _(source):
            def visit(listed, rank):
                row = block_ref[source * listed_count + listed] - scen * rows_own
                mine = (row >= 0) & (row < rows_own)
                scenario = source * listed_count + listed // spread * spread

                @pl.when(mine)
                def _():
                    for slot in range(slots):
                        col = block_ref[scenario + link * slots + slot] - first_col
                        entry = (source * limit + rank) * slots + slot
                        owner = col // per_chunk
                        held = count_ref[owner]
                        list_ref[owner, held] = entry
                        count_ref[owner] = held + 1
                        row_ref[entry] = row
                        col_ref[entry] = col

                @pl.when(mine & (block_ref[scenario] == 0))
                def _():
                    scales = column_scales_ref[source, :, :tile]
                    picked = lax.broadcasted_iota(I32, scales.shape, 0) == rank
                    scale = jnp.sum(jnp.where(picked, scales, 0.0), axis=0, keepdims=True)
                    codes = column_ref[source, pl.ds(pl.multiple_of(rank * tile, tile), tile), :]
                    down = pl.ds(pl.multiple_of(row * tile, tile), tile)
                    sums_ref[down, :] += codes.astype(I32).astype(F32) * scale

                return rank + mine.astype(I32)

            lax.fori_loop(0, listed_count, visit, jnp.int32(0))

        group = min(4, rows_own) * tile
        for start in range(0, rows_own * tile, group):
            at = slice(start, start + group)
            solved = lax.dot_general(
                sums_ref[at, :],
                inverse_ref[...],
                (((1,), (1,)), ((), ())),
                precision=HIGHEST,
                preferred_element_type=F32,
            )
            if start == 0:
                top = jnp.where(scen == 0, lower_ref[...], solved[:tile])
                solved = jnp.concatenate([top, solved[tile:]], axis=0)
            panel_ref[at, :] = solved
            high, low = split(-solved)
            left_ref[at, :tile] = high
            left_ref[at, tile : 2 * tile] = low
            left_ref[at, 2 * tile :] = high

    part = jnp.dot(
        inverse_ref[...],
        raw_ref[:, pl.ds(pl.multiple_of(step * chunk, chunk), chunk)],
        precision=HIGHEST,
        preferred_element_type=F32,
    )
    is_lead = (link == 0) & (step == 0)
    top = jnp.where(is_lead, lower_ref[...].T, part[:, :tile])
    part = jnp.concatenate([top, part[:, tile:]], axis=1) if per_chunk > 1 else top
    high, low = split(part)
    right = jnp.concatenate([high, high, low], axis=0)
    strip = min(8, rows_own) * tile
    for at in range(0, rows_own * tile, strip):
        trailing_ref[at : at + strip, :] = jnp.dot(
            left_ref[at : at + strip, :], right, preferred_element_type=F32
        )

    @pl.loop(0, count_ref[step])
    def _(place):
        entry = list_ref[step, place]
        listed = entry // slots
        slot = entry - listed * slots
        source = listed // limit
        rank = listed - source * limit
        col = col_ref[entry] - step * per_chunk
        down = pl.ds(pl.multiple_of(row_ref[entry] * tile, tile), tile)
        along = pl.ds(pl.multiple_of(col * tile, tile), tile)
        from_rows = pl.ds(pl.multiple_of(rank * tile, tile), tile)
        from_lanes = pl.ds(pl.multiple_of(slot * tile, tile), tile)
        scales = scales_ref[source, :, from_lanes]
        picked = lax.broadcasted_iota(I32, scales.shape, 0) == rank
        scale = jnp.sum(jnp.where(picked, scales, 0.0), axis=0, keepdims=True)
        codes = arrived_ref[source, slot, from_rows, :]
        trailing_ref[down, along] += codes.astype(I32).astype(F32) * scale

    unit = lax.broadcasted_iota(I32, (tile, tile), 0) == lax.broadcasted_iota(
        I32, (tile, tile), 1
    )
    for col in range(per_chunk):
        row = first_col + step * per_chunk + col - scen * rows_own

        @pl.when((row >= 0) & (row < rows_own))
        def _():
            down = pl.ds(pl.multiple_of(row * tile, tile), tile)
            trailing_ref[down, col * tile : (col + 1) * tile] += jnp.where(
                unit, diag_ref[pl.ds(row, 1), :], 0.0
            )


def finish(place, blocks, arrays, spread, limit, width):
    lower, diag = arrays[6], arrays[8]
    entries = arrays[0].shape[0] * arrays[0].shape[1] * limit
    tile = lower.shape[0]
    rows = diag.shape[0] * tile
    chunk = min(512, width)
    return pl.pallas_call(
        lambda *refs: finish_kernel(limit, spread, *refs),
        grid_spec=pltpu.PrefetchScalarGridSpec(
            num_scalar_prefetch=2,
            grid=(width // chunk,),
            in_specs=[VMEM] * len(arrays),
            out_specs=[
                pl.BlockSpec((rows, tile), lambda c, *_: (0, 0)),
                pl.BlockSpec((rows, chunk), lambda c, *_: (0, c)),
            ],
            scratch_shapes=[
                pltpu.VMEM((rows, 3 * tile), BF16),
                pltpu.VMEM((tile, width), F32),
                pltpu.VMEM((rows, tile), F32),
                pltpu.SMEM((width // chunk, entries), I32),
                pltpu.SMEM((entries,), I32),
                pltpu.SMEM((entries,), I32),
                pltpu.SMEM((width // chunk,), I32),
            ],
        ),
        out_shape=(
            jax.ShapeDtypeStruct((rows, tile), F32),
            jax.ShapeDtypeStruct((rows, width), F32),
        ),
        name="finish",
        compiler_params=pltpu.CompilerParams(vmem_limit_bytes=48 * MIB),
    )(place, blocks, *arrays)


def per_device(factor_inv, coupling, first_diag, pattern):
    rows_own, tile = first_diag.shape
    scen_count = lax.axis_size("scen")
    link_count = lax.axis_size("link")
    scen_pos = lax.axis_index("scen")
    link_pos = lax.axis_index("link")
    per_link = rows_own * scen_count // link_count
    scen_here, spread = pattern.shape
    width = coupling.shape[2]
    slots = width // tile

    padded = jnp.pad(pattern, ((0, 8 - scen_here), (0, 128 - spread)))
    gathered, corner, patterns = gather(
        factor_inv, coupling, first_diag, padded, scen_count, link_count
    )
    patterns = patterns[:, :scen_here, :spread]

    picks = scen_here * slots
    owners_here = max(1, per_link // rows_own)
    limit = max(1, (picks + owners_here - 1) // owners_here)
    coded, scales = contribute(
        pattern.reshape(-1),
        link_pos[None].astype(I32),
        gathered,
        tile,
        scen_count,
        rows_own,
        limit,
    )
    arrays = exchange(coded, scales, corner, link_count) + (first_diag,)
    place = jnp.stack([scen_pos, link_pos]).astype(I32)
    return finish(place, patterns.reshape(-1), arrays, spread, limit, per_link * tile)


def solution(mesh):
    in_specs = (P("scen", None, None), P("scen", None, "link"), P("scen", None), P("scen", None))
    out_specs = (P("scen", None), P("scen", "link"))
    return jax.shard_map(
        per_device, mesh=mesh, in_specs=in_specs, out_specs=out_specs, check_vma=False
    )
```

```python
import jax
import jax.numpy as jnp
from jax import lax
from jax.experimental import pallas as pl
from jax.experimental.pallas import tpu as pltpu
from jax.sharding import PartitionSpec as P

F32 = jnp.float32
BF16 = jnp.bfloat16
I32 = jnp.int32
I16 = jnp.int16
HIGHEST = lax.Precision.HIGHEST
MESH = pl.DeviceIdType.MESH
VMEM = pl.BlockSpec(memory_space=pltpu.VMEM)
ANY = pl.BlockSpec(memory_space=pl.ANY)
MIB = 2**20
LEVELS = 32767.0


def factor(work):
    size = work.shape[0]
    inverse = (
        lax.broadcasted_iota(I32, (size, size), 0) == lax.broadcasted_iota(I32, (size, size), 1)
    ).astype(F32)
    upper_rows, inverse_rows = [], []
    base = 0
    for j in range(size):
        start = j // 8 * 8
        if start > base:
            work, inverse, base = work[start - base :], inverse[start - base :], start
        k = j - base
        column = work[:, j : j + 1]
        pivot = column[k : k + 1]
        row, inverse_row = work[k : k + 1], inverse[k : k + 1]
        scale = 1.0 / jnp.sqrt(pivot)
        upper_rows.append(row * scale)
        inverse_rows.append(inverse_row * scale)
        if j + 1 < size:
            below = lax.broadcasted_iota(I32, (size - base, 1), 0) > k
            ratio = jnp.where(below, column * (1.0 / pivot), 0.0)
            work = work - ratio * row
            inverse = inverse - ratio * inverse_row
    return jnp.concatenate(upper_rows, axis=0), jnp.concatenate(inverse_rows, axis=0)


def factor_into(corner_ref, lower_ref, inverse_ref):
    upper, inverse = factor(corner_ref[...])
    size = upper.shape[0]
    keep = lax.broadcasted_iota(I32, (size, size), 0) <= lax.broadcasted_iota(
        I32, (size, size), 1
    )
    lower_ref[...] = jnp.where(keep, upper, 0.0).T
    inverse_ref[...] = inverse


def greet(scen_count, link_count):
    scen, link = lax.axis_index("scen"), lax.axis_index("link")
    barrier = pltpu.get_barrier_semaphore()

    @pl.loop(1, scen_count)
    def _(step):
        pl.semaphore_signal(
            barrier,
            inc=1,
            device_id={"scen": lax.rem(scen + step, scen_count)},
            device_id_type=MESH,
        )

    for step in range(1, link_count):
        pl.semaphore_signal(
            barrier,
            inc=1,
            device_id={"link": lax.rem(link + step, link_count)},
            device_id_type=MESH,
        )
    pl.semaphore_wait(barrier, scen_count + link_count - 2)


def gather_kernel(
    scen_count,
    link_count,
    factor_ref,
    coupling_ref,
    diag_ref,
    pattern_ref,
    gathered_ref,
    corner_ref,
    patterns_ref,
    held_ref,
    columns_ref,
    first_ref,
    own_ref,
    shares_ref,
    held_sem,
    kept_sem,
    scen_send,
    scen_recv,
    slab_send,
    slab_recv,
    link_send,
    link_recv,
):
    scen, link = lax.axis_index("scen"), lax.axis_index("link")
    scen_here, depth, width = coupling_ref.shape
    tile = corner_ref.shape[0]
    halves = 2
    rows = depth // halves
    half = link_count // 2
    twin = link + 1 - 2 * lax.rem(link, 2)
    across = lax.rem(link + half, link_count)

    def fetch(which, scenario):
        src, dst = ((factor_ref, held_ref), (coupling_ref, columns_ref))[which]
        return pltpu.make_async_copy(
            src.at[scenario], dst.at[scenario], held_sem.at[which, scenario]
        )

    def keep(scenario):
        return pltpu.make_async_copy(
            own_ref.at[scenario], gathered_ref.at[link, scenario], kept_sem.at[scenario]
        )

    first = pltpu.make_async_copy(diag_ref, first_ref, held_sem.at[2, 0])
    for scenario in range(scen_here):
        for which in (1, 0):
            fetch(which, scenario).start()
    first.start()
    greet(scen_count, link_count)

    def share_copy(source, peer):
        return pltpu.make_async_remote_copy(
            src_ref=shares_ref.at[scen],
            dst_ref=shares_ref.at[source],
            send_sem=scen_send.at[0, peer],
            recv_sem=scen_recv.at[0, source],
            device_id={"scen": peer},
            device_id_type=MESH,
        )

    def pattern_copy(source, peer):
        return pltpu.make_async_remote_copy(
            src_ref=pattern_ref,
            dst_ref=patterns_ref.at[source],
            send_sem=scen_send.at[1, peer],
            recv_sem=scen_recv.at[1, source],
            device_id={"scen": peer},
            device_id_type=MESH,
        )

    def corner_copy(target):
        return pltpu.make_async_remote_copy(
            src_ref=corner_ref,
            dst_ref=corner_ref,
            send_sem=link_send.at[target],
            recv_sem=link_recv,
            device_id={"link": target},
            device_id_type=MESH,
        )

    def slab_copy(way, scenario, piece, source, target):
        down = pl.ds(piece * rows, rows)
        at = gathered_ref.at[source, scenario, down]
        return pltpu.make_async_remote_copy(
            src_ref=at if way == 2 else own_ref.at[scenario, down],
            dst_ref=at,
            send_sem=slab_send.at[way, scenario, piece],
            recv_sem=slab_recv.at[way, scenario, piece],
            device_id={"link": target},
            device_id_type=MESH,
        )

    def over_peers(act):
        @pl.loop(1, scen_count)
        def _(step):
            act(lax.rem(scen + step, scen_count))

    for scenario in range(scen_here):
        fetch(1, scenario).wait()
        fetch(0, scenario).wait()
        for piece in range(halves):
            strip = rows // 2
            for part in range(2):
                down = slice(piece * rows + part * strip, piece * rows + (part + 1) * strip)
                own_ref[scenario, down, :] = jnp.dot(
                    held_ref[scenario, down, :],
                    columns_ref[scenario],
                    preferred_element_type=F32,
                ).astype(BF16)
            slab_copy(1, scenario, piece, link, across).start()
            slab_copy(0, scenario, piece, link, twin).start()
        keep(scenario).start()
        if scenario == 0:
            first.wait()

            @pl.when(link == 0)
            def _():
                lead = own_ref[0, :, :tile]
                share = lax.dot_general(
                    lead, lead, (((0,), (0,)), ((), ())), preferred_element_type=F32
                )
                unit = lax.broadcasted_iota(I32, (tile, tile), 0) == lax.broadcasted_iota(
                    I32, (tile, tile), 1
                )
                shares_ref[scen] = share + jnp.where(unit & (scen == 0), first_ref[0:1, :], 0.0)
                over_peers(lambda peer: share_copy(scen, peer).start())

    patterns_ref[scen] = pattern_ref[...]
    over_peers(lambda peer: pattern_copy(scen, peer).start())

    @pl.when(link == 0)
    def _():
        over_peers(lambda peer: share_copy(peer, peer).wait_recv())
        corner_ref[...] = shares_ref[0]

        @pl.loop(1, scen_count)
        def _(source):
            corner_ref[...] += shares_ref[source]

        for target in range(1, link_count):
            corner_copy(target).start()

    pieces = [(scenario, piece) for scenario in range(scen_here) for piece in range(halves)]
    for scenario, piece in pieces:
        slab_copy(1, scenario, piece, across, across).wait_recv()
        slab_copy(2, scenario, piece, across, twin).start()
    beyond = lax.rem(twin + half, link_count)
    for scenario, piece in pieces:
        slab_copy(0, scenario, piece, twin, twin).wait_recv()
        slab_copy(2, scenario, piece, beyond, twin).wait_recv()
    for scenario, piece in pieces:
        slab_copy(0, scenario, piece, link, twin).wait_send()
        slab_copy(1, scenario, piece, link, across).wait_send()
        slab_copy(2, scenario, piece, across, twin).wait_send()

    @pl.when(link == 0)
    def _():
        over_peers(lambda peer: share_copy(scen, peer).wait_send())
        for target in range(1, link_count):
            corner_copy(target).wait_send()

    for scenario in range(scen_here):
        keep(scenario).wait()

    def finish_pattern(peer):
        pattern_copy(scen, peer).wait_send()
        pattern_copy(peer, peer).wait_recv()

    over_peers(finish_pattern)

    @pl.when(link != 0)
    def _():
        corner_copy(0).wait_recv()


def gather(factor_inv, coupling, diag, pattern, scen_count, link_count):
    tile = diag.shape[1]
    dma = pltpu.SemaphoreType.DMA
    pieces = (3, coupling.shape[0], 2)
    return pl.pallas_call(
        lambda *refs: gather_kernel(scen_count, link_count, *refs),
        out_shape=(
            jax.ShapeDtypeStruct((link_count,) + coupling.shape, BF16),
            jax.ShapeDtypeStruct((tile, tile), F32),
            jax.ShapeDtypeStruct((scen_count,) + pattern.shape, I32),
        ),
        in_specs=[ANY, ANY, ANY, VMEM],
        out_specs=(ANY, VMEM, VMEM),
        scratch_shapes=[
            pltpu.VMEM(factor_inv.shape, BF16),
            pltpu.VMEM(coupling.shape, BF16),
            pltpu.VMEM(diag.shape, F32),
            pltpu.VMEM(coupling.shape, BF16),
            pltpu.VMEM((scen_count, tile, tile), F32),
            dma((3, coupling.shape[0])),
            dma((coupling.shape[0],)),
            dma((2, scen_count)),
            dma((2, scen_count)),
            dma(pieces),
            dma(pieces),
            dma((link_count,)),
            dma,
        ],
        name="gather",
        compiler_params=pltpu.CompilerParams(
            collective_id=0, has_side_effects=True, vmem_limit_bytes=60 * MIB
        ),
    )(factor_inv, coupling, diag, pattern)


def contribute_kernel(
    limit, clear, target_ref, link_ref, rows_ref, own_ref, coded_ref, scales_ref
):
    scenario, piece = pl.program_id(0), pl.program_id(1)
    tile = coded_ref.shape[3]
    slots = coded_ref.shape[1]
    spread = slots * pl.num_programs(1)
    if clear:

        @pl.when((scenario == 0) & (piece == 0))
        def _():
            coded_ref[...] = jnp.zeros_like(coded_ref)
            scales_ref[...] = jnp.zeros_like(scales_ref)

    product = lax.dot_general(
        rows_ref[0, 0], own_ref[0, 0], (((0,), (0,)), ((), ())), preferred_element_type=F32
    )
    for slab in range(slots):
        values = product[slab * tile : (slab + 1) * tile]
        target = target_ref[scenario * spread + piece * slots + slab]
        dest = target // limit
        rank = target - dest * limit
        peak = jnp.max(jnp.abs(values), axis=0, keepdims=True)
        gain = jnp.where(peak > 1e-30, LEVELS / jnp.maximum(peak, 1e-30), 0.0)
        code = jnp.round(values * gain).astype(I32).astype(I16)
        scales_ref[dest, pl.ds(rank, 1), :] = peak * (1.0 / LEVELS)
        for slot in range(slots):
            coded_ref[dest, slot, pl.ds(pl.multiple_of(rank * tile, tile), tile), :] = code[
                :, slot * tile : (slot + 1) * tile
            ]


def contribute(target, link, gathered, tile, scen_count, limit):
    link_count, scen_here, depth, width = gathered.shape
    slots = width // tile
    clear = scen_count * limit > target.shape[0]
    return pl.pallas_call(
        lambda *refs: contribute_kernel(limit, clear, *refs),
        grid_spec=pltpu.PrefetchScalarGridSpec(
            num_scalar_prefetch=2,
            grid=(scen_here, link_count),
            in_specs=[
                pl.BlockSpec((1, 1, depth, width), lambda i, j, *_: (j, i, 0, 0)),
                pl.BlockSpec((1, 1, depth, width), lambda i, j, _, link: (link[0], i, 0, 0)),
            ],
            out_specs=[
                pl.BlockSpec((scen_count, slots, limit * tile, tile), lambda i, j, *_: (0, 0, 0, 0)),
                pl.BlockSpec((scen_count, 8, width), lambda i, j, *_: (0, 0, 0)),
            ],
        ),
        out_shape=(
            jax.ShapeDtypeStruct((scen_count, slots, limit * tile, tile), I16),
            jax.ShapeDtypeStruct((scen_count, 8, width), F32),
        ),
        name="contribute",
        compiler_params=pltpu.CompilerParams(vmem_limit_bytes=32 * MIB),
    )(target, link, gathered, gathered)


def exchange_kernel(
    scen_count,
    link_count,
    coded_ref,
    scales_ref,
    corner_ref,
    arrived_ref,
    arrived_scales_ref,
    lower_ref,
    side_ref,
    down_ref,
    inverse_ref,
    lead_ref,
    lead_scales_ref,
    column_ref,
    column_scales_ref,
    send_sem,
    recv_sem,
    local_sem,
    lead_send,
    lead_recv,
    link_send,
    link_recv,
):
    scen, link = lax.axis_index("scen"), lax.axis_index("link")
    tile = coded_ref.shape[3]
    slots = coded_ref.shape[1]
    greet(scen_count, link_count)

    def ends(kind, source, dest):
        if kind == 0:
            return scales_ref.at[dest], arrived_scales_ref.at[source]
        return coded_ref.at[dest, kind - 1], arrived_ref.at[source, kind - 1]

    def copy(kind, source, peer):
        src, dst = ends(kind, source, peer)
        return pltpu.make_async_remote_copy(
            src_ref=src,
            dst_ref=dst,
            send_sem=send_sem.at[kind, peer],
            recv_sem=recv_sem.at[kind, source],
            device_id={"scen": peer},
            device_id_type=MESH,
        )

    def keep(kind):
        src, dst = ends(kind, scen, scen)
        return pltpu.make_async_copy(src, dst, local_sem.at[kind])

    def over_peers(act):
        @pl.loop(1, scen_count)
        def _(step):
            act(lax.rem(scen + step, scen_count))

    first, later = (0, 1), tuple(range(2, slots + 1))

    def start_first(peer):
        for kind in first:
            copy(kind, scen, peer).start()

    def start_later(peer):
        for kind in later:
            copy(kind, scen, peer).start()

    def finish_send(kinds):
        def act(peer):
            for kind in kinds:
                copy(kind, scen, peer).wait_send()

        return act

    def finish_recv(kinds):
        def act(peer):
            for kind in kinds:
                copy(kind, peer, peer).wait_recv()

        return act

    line = scen_count // 2
    spot, side = scen // 2, lax.rem(scen, 2)
    pair = scen + 1 - 2 * side

    def lead_copies(way, block, target):
        return [
            pltpu.make_async_remote_copy(
                src_ref=ref.at[block],
                dst_ref=ref.at[block],
                send_sem=lead_send.at[which, way, block],
                recv_sem=lead_recv.at[which, block],
                device_id={"scen": target},
                device_id_type=MESH,
            )
            for which, ref in enumerate((lead_ref, lead_scales_ref))
        ]

    def lead_wait(block):
        for one in lead_copies(2, block, pair):
            one.wait_recv()

    def lead_pass(block, left, right, act):
        @pl.when(left & (spot > 0))
        def _():
            for one in lead_copies(0, block, lax.rem(scen + scen_count - 2, scen_count)):
                act(one)

        @pl.when(right & (spot < line - 1))
        def _():
            for one in lead_copies(1, block, lax.rem(scen + 2, scen_count)):
                act(one)

        for one in lead_copies(2, block, pair):
            act(one)

    def begin(one):
        one.start()

    def end(one):
        one.wait_send()

    def over_line(act, arriving):
        @pl.loop(1, line)
        def _(step):
            @pl.when(spot - step >= 0)
            def _():
                block = scen - 2 * step
                if arriving:
                    lead_wait(block)
                lead_pass(block, False, True, act)

            @pl.when(spot + step < line)
            def _():
                block = scen + 2 * step
                if arriving:
                    lead_wait(block)
                lead_pass(block, True, False, act)

    over_peers(start_first)
    lead_ref[scen] = coded_ref[0, :, :tile, :]
    lead_scales_ref[scen] = scales_ref[0]
    lead_pass(scen, True, True, begin)
    for kind in first + later:
        keep(kind).start()
    factor_into(corner_ref, lower_ref, inverse_ref)
    over_peers(finish_send(first))
    over_peers(start_later)
    for kind in first + later:
        keep(kind).wait()

    half = link_count // 2

    def column_copies(source, target, way, relayed):
        pairs = (
            (column_ref if relayed else arrived_ref.at[:, 0], column_ref),
            (column_scales_ref if relayed else arrived_scales_ref, column_scales_ref),
        )
        return [
            pltpu.make_async_remote_copy(
                src_ref=src.at[source],
                dst_ref=dst.at[source],
                send_sem=link_send.at[which, way, source],
                recv_sem=link_recv.at[which, source],
                device_id={"link": target},
                device_id_type=MESH,
            )
            for which, (src, dst) in enumerate(pairs)
        ]

    def column_out(source):
        for target in (half,) + tuple(range(1, half)):
            for one in column_copies(source, target, target % half, False):
                one.start()

    def column_out_end(source):
        for target in (half,) + tuple(range(1, half)):
            for one in column_copies(source, target, target % half, False):
                one.wait_send()

    @pl.when(link == 0)
    def _():
        column_out(scen)

        @pl.loop(1, scen_count)
        def _(step):
            peer = lax.rem(scen + step, scen_count)
            finish_recv(first)(peer)
            column_out(peer)

    over_line(begin, True)

    @pl.when(link == 0)
    def _():
        column_ref[...] = arrived_ref[:, 0]
        column_scales_ref[...] = arrived_scales_ref[...]

        @pl.loop(0, scen_count)
        def _(source):
            column_out_end(source)

    @pl.when(link != 0)
    def _():
        over_peers(finish_recv(first))

        @pl.loop(0, scen_count)
        def _(step):
            source = lax.rem(scen + step, scen_count)
            for one in column_copies(source, 0, 0, True):
                one.wait_recv()

            @pl.when(link == half)
            def _():
                for target in range(half + 1, link_count):
                    for one in column_copies(source, target, target - half, True):
                        one.start()

        @pl.when(link == half)
        def _():
            @pl.loop(0, scen_count)
            def _(source):
                for target in range(half + 1, link_count):
                    for one in column_copies(source, target, target - half, True):
                        one.wait_send()

    @pl.loop(0, line)
    def _(step):
        lead_wait(2 * step + 1 - side)

    @pl.loop(0, scen_count)
    def _(source):
        for slot in range(slots):
            at = slice(slot * tile, (slot + 1) * tile)
            side_ref[source, slot] = jnp.dot(
                inverse_ref[...],
                lead_ref[source, slot].astype(I32).astype(F32) * lead_scales_ref[source, 0:1, at],
                precision=HIGHEST,
                preferred_element_type=F32,
            )
        for rank in range(column_ref.shape[1] // tile):
            at = slice(rank * tile, (rank + 1) * tile)
            codes = column_ref[source, at, :].astype(I32).astype(F32)
            down_ref[source, at, :] = lax.dot_general(
                codes * column_scales_ref[source, rank : rank + 1, :tile],
                inverse_ref[...],
                (((1,), (1,)), ((), ())),
                precision=HIGHEST,
                preferred_element_type=F32,
            )

    lead_pass(scen, True, True, end)
    over_line(end, False)
    over_peers(finish_recv(later))
    over_peers(finish_send(later))


def exchange(coded, scales, corner, link_count):
    tile = corner.shape[0]
    scen_count, slots, rows = coded.shape[:3]
    kinds = slots + 1
    dma = pltpu.SemaphoreType.DMA
    return pl.pallas_call(
        lambda *refs: exchange_kernel(scen_count, link_count, *refs),
        out_shape=(
            jax.ShapeDtypeStruct(coded.shape, I16),
            jax.ShapeDtypeStruct(scales.shape, F32),
            jax.ShapeDtypeStruct((tile, tile), F32),
            jax.ShapeDtypeStruct((scen_count, slots, tile, tile), F32),
            jax.ShapeDtypeStruct((scen_count, rows, tile), F32),
        ),
        in_specs=[VMEM, VMEM, VMEM],
        out_specs=(VMEM,) * 5,
        scratch_shapes=[
            pltpu.VMEM((tile, tile), F32),
            pltpu.VMEM((scen_count, slots, tile, tile), I16),
            pltpu.VMEM(scales.shape, F32),
            pltpu.VMEM((scen_count, rows, tile), I16),
            pltpu.VMEM(scales.shape, F32),
            dma((kinds, scen_count)),
            dma((kinds, scen_count)),
            dma((kinds,)),
            dma((2, 3, scen_count)),
            dma((2, scen_count)),
            dma((2, max(1, link_count // 2), scen_count)),
            dma((2, scen_count)),
        ],
        name="exchange",
        compiler_params=pltpu.CompilerParams(
            collective_id=1, has_side_effects=True, vmem_limit_bytes=48 * MIB
        ),
    )(coded, scales, corner)


def split(value):
    high = value.astype(BF16)
    return high, (value - high.astype(F32)).astype(BF16)


def finish_kernel(
    limit,
    place_ref,
    row_label_ref,
    col_label_ref,
    lead_label_ref,
    column_label_ref,
    arrived_ref,
    scales_ref,
    lower_ref,
    side_ref,
    down_ref,
    diag_ref,
    panel_ref,
    trailing_ref,
    left_ref,
    raw_ref,
    list_ref,
    count_ref,
):
    tile = lower_ref.shape[0]
    chunk = trailing_ref.shape[1]
    slots = arrived_ref.shape[1]
    rows_own = diag_ref.shape[0]
    step = pl.program_id(0)
    per_chunk = chunk // tile
    scen, link = place_ref[0], place_ref[1]
    first_col = link * per_chunk * pl.num_programs(0)

    @pl.when(step == 0)
    def _():
        raw_ref[...] = jnp.zeros_like(raw_ref)
        panel_ref[...] = jnp.zeros_like(panel_ref)

        @pl.loop(0, side_ref.shape[0])
        def _(source):
            for slot in range(slots):
                at = pl.multiple_of(lead_label_ref[source * slots + slot] * tile, tile)
                raw_ref[:, pl.ds(at, tile)] += side_ref[source, slot]
            for rank in range(limit):
                label = column_label_ref[source * limit + rank]

                @pl.when(label >= 0)
                def _():
                    at = pl.ds(pl.multiple_of(label * tile, tile), tile)
                    panel_ref[at, :] += down_ref[source, rank * tile : (rank + 1) * tile, :]

        @pl.when(link == 0)
        def _():
            raw_ref[:, :tile] = lower_ref[...].T

        @pl.when(scen == 0)
        def _():
            panel_ref[:tile, :] = lower_ref[...]

        high, low = split(-panel_ref[...])
        left_ref[:, :tile] = high
        left_ref[:, tile : 2 * tile] = low
        left_ref[:, 2 * tile :] = high

        for other in range(count_ref.shape[0]):
            count_ref[other] = 0

        @pl.loop(0, list_ref.shape[1])
        def _(entry):
            @pl.when(row_label_ref[entry // slots] >= 0)
            def _():
                owner = col_label_ref[entry] // per_chunk
                held = count_ref[owner]
                list_ref[owner, held] = entry
                count_ref[owner] = held + 1

    part = raw_ref[:, pl.ds(pl.multiple_of(step * chunk, chunk), chunk)]
    high, low = split(part)
    right = jnp.concatenate([high, high, low], axis=0)
    strip = min(8, rows_own) * tile
    for at in range(0, rows_own * tile, strip):
        trailing_ref[at : at + strip, :] = jnp.dot(
            left_ref[at : at + strip, :], right, preferred_element_type=F32
        )

    @pl.loop(0, count_ref[step])
    def _(place):
        entry = list_ref[step, place]
        listed = entry // slots
        slot = entry - listed * slots
        source = listed // limit
        rank = listed - source * limit
        col = col_label_ref[entry] - step * per_chunk
        down = pl.ds(pl.multiple_of(row_label_ref[listed] * tile, tile), tile)
        along = pl.ds(pl.multiple_of(col * tile, tile), tile)
        from_rows = pl.ds(pl.multiple_of(rank * tile, tile), tile)
        from_lanes = pl.ds(pl.multiple_of(slot * tile, tile), tile)
        scales = scales_ref[source, :, from_lanes]
        picked = lax.broadcasted_iota(I32, scales.shape, 0) == rank
        scale = jnp.sum(jnp.where(picked, scales, 0.0), axis=0, keepdims=True)
        codes = arrived_ref[source, slot, from_rows, :]
        trailing_ref[down, along] += codes.astype(I32).astype(F32) * scale

    unit = lax.broadcasted_iota(I32, (tile, tile), 0) == lax.broadcasted_iota(
        I32, (tile, tile), 1
    )
    for col in range(per_chunk):
        row = first_col + step * per_chunk + col - scen * rows_own

        @pl.when((row >= 0) & (row < rows_own))
        def _():
            down = pl.ds(pl.multiple_of(row * tile, tile), tile)
            trailing_ref[down, col * tile : (col + 1) * tile] += jnp.where(
                unit, diag_ref[pl.ds(row, 1), :], 0.0
            )


def finish(labels, arrays, limit, width):
    lower, diag = arrays[2], arrays[5]
    entries = labels[2].shape[0]
    tile = lower.shape[0]
    rows = diag.shape[0] * tile
    chunk = min(512, width)
    return pl.pallas_call(
        lambda *refs: finish_kernel(limit, *refs),
        grid_spec=pltpu.PrefetchScalarGridSpec(
            num_scalar_prefetch=5,
            grid=(width // chunk,),
            in_specs=[VMEM] * len(arrays),
            out_specs=[
                pl.BlockSpec((rows, tile), lambda c, *_: (0, 0)),
                pl.BlockSpec((rows, chunk), lambda c, *_: (0, c)),
            ],
            scratch_shapes=[
                pltpu.VMEM((rows, 3 * tile), BF16),
                pltpu.VMEM((tile, width), F32),
                pltpu.SMEM((width // chunk, entries), I32),
                pltpu.SMEM((width // chunk,), I32),
            ],
        ),
        out_shape=(
            jax.ShapeDtypeStruct((rows, tile), F32),
            jax.ShapeDtypeStruct((rows, width), F32),
        ),
        name="finish",
        compiler_params=pltpu.CompilerParams(vmem_limit_bytes=48 * MIB),
    )(*labels, *arrays)


def per_device(factor_inv, coupling, first_diag, pattern):
    rows_own, tile = first_diag.shape
    scen_count = lax.axis_size("scen")
    link_count = lax.axis_size("link")
    scen_pos = lax.axis_index("scen")
    link_pos = lax.axis_index("link")
    per_link = rows_own * scen_count // link_count
    scen_here, spread = pattern.shape
    width = coupling.shape[2]
    slots = width // tile

    padded = jnp.pad(pattern, ((0, 8 - scen_here), (0, 128 - spread)))
    gathered, corner, patterns = gather(
        factor_inv, coupling, first_diag, padded, scen_count, link_count
    )
    patterns = patterns[:, :scen_here, :spread]

    picks = scen_here * slots
    owners_here = max(1, per_link // rows_own)
    limit = max(1, (picks + owners_here - 1) // owners_here)
    listed = jnp.arange(scen_here * spread, dtype=I32)

    def targets(blocks):
        owners = blocks // rows_own
        earlier = (owners[..., :, None] == owners[..., None, :]) & (
            listed[None, :] < listed[:, None]
        )
        return owners * limit + jnp.sum(earlier.astype(I32), axis=-1)

    coded, scales = contribute(
        targets(pattern.reshape(-1)), link_pos[None].astype(I32), gathered, tile, scen_count, limit
    )

    blocks = patterns.reshape(scen_count, scen_here * spread)
    places = scen_pos * limit + jnp.arange(limit, dtype=I32)
    hit = targets(blocks)[:, :, None] == places[None, None, :]
    rows_from = blocks - scen_pos * rows_own + 1
    row_labels = jnp.sum(jnp.where(hit, rows_from[:, :, None], 0), axis=1) - 1
    leading = jnp.repeat(patterns[:, :, 0] == 0, spread, axis=1)
    column_labels = (
        jnp.sum(jnp.where(hit & leading[:, :, None], rows_from[:, :, None], 0), axis=1) - 1
    )
    own_cols = (
        lax.dynamic_slice_in_dim(patterns, link_pos * slots, slots, 2) - link_pos * per_link
    )
    slab_cols = jnp.repeat(own_cols, spread, axis=1)
    col_labels = jnp.sum(jnp.where(hit[:, :, :, None], slab_cols[:, :, None, :], 0), axis=1)
    lead_labels = own_cols[:, 0, :]

    arrays = exchange(coded, scales, corner, link_count) + (first_diag,)
    place = jnp.stack([scen_pos, link_pos]).astype(I32)
    labels = (place,) + tuple(
        one.reshape(-1) for one in (row_labels, col_labels, lead_labels, column_labels)
    )
    return finish(labels, arrays, limit, per_link * tile)


def solution(mesh):
    in_specs = (P("scen", None, None), P("scen", None, "link"), P("scen", None), P("scen", None))
    out_specs = (P("scen", None), P("scen", "link"))
    return jax.shard_map(
        per_device, mesh=mesh, in_specs=in_specs, out_specs=out_specs, check_vma=False
    )
```

```python
import jax
import jax.numpy as jnp
from jax import lax
from jax.experimental import pallas as pl
from jax.experimental.pallas import tpu as pltpu
from jax.sharding import PartitionSpec as P

F32 = jnp.float32
BF16 = jnp.bfloat16
I32 = jnp.int32
I16 = jnp.int16
HIGHEST = lax.Precision.HIGHEST
MESH = pl.DeviceIdType.MESH
VMEM = pl.BlockSpec(memory_space=pltpu.VMEM)
ANY = pl.BlockSpec(memory_space=pl.ANY)
MIB = 2**20
LEVELS = 32767.0


def factor(work):
    size = work.shape[0]
    inverse = (
        lax.broadcasted_iota(I32, (size, size), 0) == lax.broadcasted_iota(I32, (size, size), 1)
    ).astype(F32)
    upper_rows, inverse_rows = [], []
    base = 0
    for j in range(size):
        start = j // 8 * 8
        if start > base:
            work, inverse, base = work[start - base :], inverse[start - base :], start
        k = j - base
        column = work[:, j : j + 1]
        pivot = column[k : k + 1]
        row, inverse_row = work[k : k + 1], inverse[k : k + 1]
        scale = 1.0 / jnp.sqrt(pivot)
        upper_rows.append(row * scale)
        inverse_rows.append(inverse_row * scale)
        if j + 1 < size:
            below = lax.broadcasted_iota(I32, (size - base, 1), 0) > k
            ratio = jnp.where(below, column * (1.0 / pivot), 0.0)
            work = work - ratio * row
            inverse = inverse - ratio * inverse_row
    return jnp.concatenate(upper_rows, axis=0), jnp.concatenate(inverse_rows, axis=0)


def factor_into(corner_ref, lower_ref, inverse_ref):
    upper, inverse = factor(corner_ref[...])
    size = upper.shape[0]
    keep = lax.broadcasted_iota(I32, (size, size), 0) <= lax.broadcasted_iota(
        I32, (size, size), 1
    )
    lower_ref[...] = jnp.where(keep, upper, 0.0).T
    inverse_ref[...] = inverse


def greet(scen_count, link_count):
    scen, link = lax.axis_index("scen"), lax.axis_index("link")
    barrier = pltpu.get_barrier_semaphore()

    @pl.loop(1, scen_count)
    def _(step):
        pl.semaphore_signal(
            barrier,
            inc=1,
            device_id={"scen": lax.rem(scen + step, scen_count)},
            device_id_type=MESH,
        )

    for step in range(1, link_count):
        pl.semaphore_signal(
            barrier,
            inc=1,
            device_id={"link": lax.rem(link + step, link_count)},
            device_id_type=MESH,
        )
    pl.semaphore_wait(barrier, scen_count + link_count - 2)


def gather_kernel(
    scen_count,
    link_count,
    factor_ref,
    coupling_ref,
    diag_ref,
    pattern_ref,
    gathered_ref,
    corner_ref,
    patterns_ref,
    held_ref,
    columns_ref,
    first_ref,
    own_ref,
    shares_ref,
    held_sem,
    kept_sem,
    scen_send,
    scen_recv,
    slab_send,
    slab_recv,
    link_send,
    link_recv,
):
    scen, link = lax.axis_index("scen"), lax.axis_index("link")
    scen_here, depth, width = coupling_ref.shape
    tile = corner_ref.shape[0]
    halves = 2
    rows = depth // halves
    half = link_count // 2
    twin = link + 1 - 2 * lax.rem(link, 2)
    across = lax.rem(link + half, link_count)

    def fetch(which, scenario):
        src, dst = ((factor_ref, held_ref), (coupling_ref, columns_ref))[which]
        return pltpu.make_async_copy(
            src.at[scenario], dst.at[scenario], held_sem.at[which, scenario]
        )

    def keep(scenario):
        return pltpu.make_async_copy(
            own_ref.at[scenario], gathered_ref.at[link, scenario], kept_sem.at[scenario]
        )

    first = pltpu.make_async_copy(diag_ref, first_ref, held_sem.at[2, 0])
    for scenario in range(scen_here):
        for which in (1, 0):
            fetch(which, scenario).start()
    first.start()
    greet(scen_count, link_count)

    def share_copy(source, peer):
        return pltpu.make_async_remote_copy(
            src_ref=shares_ref.at[scen],
            dst_ref=shares_ref.at[source],
            send_sem=scen_send.at[0, peer],
            recv_sem=scen_recv.at[0, source],
            device_id={"scen": peer},
            device_id_type=MESH,
        )

    def pattern_copy(source, peer):
        return pltpu.make_async_remote_copy(
            src_ref=pattern_ref,
            dst_ref=patterns_ref.at[source],
            send_sem=scen_send.at[1, peer],
            recv_sem=scen_recv.at[1, source],
            device_id={"scen": peer},
            device_id_type=MESH,
        )

    def corner_copy(target):
        return pltpu.make_async_remote_copy(
            src_ref=corner_ref,
            dst_ref=corner_ref,
            send_sem=link_send.at[target],
            recv_sem=link_recv,
            device_id={"link": target},
            device_id_type=MESH,
        )

    def slab_copy(way, scenario, piece, source, target):
        down = pl.ds(piece * rows, rows)
        at = gathered_ref.at[source, scenario, down]
        return pltpu.make_async_remote_copy(
            src_ref=at if way == 2 else own_ref.at[scenario, down],
            dst_ref=at,
            send_sem=slab_send.at[way, scenario, piece],
            recv_sem=slab_recv.at[way, scenario, piece],
            device_id={"link": target},
            device_id_type=MESH,
        )

    def over_peers(act):
        @pl.loop(1, scen_count)
        def _(step):
            act(lax.rem(scen + step, scen_count))

    for scenario in range(scen_here):
        fetch(1, scenario).wait()
        fetch(0, scenario).wait()
        for piece in range(halves):
            strip = rows // 2
            for part in range(2):
                down = slice(piece * rows + part * strip, piece * rows + (part + 1) * strip)
                own_ref[scenario, down, :] = jnp.dot(
                    held_ref[scenario, down, :],
                    columns_ref[scenario],
                    preferred_element_type=F32,
                ).astype(BF16)
            slab_copy(1, scenario, piece, link, across).start()
            slab_copy(0, scenario, piece, link, twin).start()
        keep(scenario).start()
        if scenario == 0:
            first.wait()

            @pl.when(link == 0)
            def _():
                lead = own_ref[0, :, :tile]
                share = lax.dot_general(
                    lead, lead, (((0,), (0,)), ((), ())), preferred_element_type=F32
                )
                unit = lax.broadcasted_iota(I32, (tile, tile), 0) == lax.broadcasted_iota(
                    I32, (tile, tile), 1
                )
                shares_ref[scen] = share + jnp.where(unit & (scen == 0), first_ref[0:1, :], 0.0)
                over_peers(lambda peer: share_copy(scen, peer).start())

    patterns_ref[scen] = pattern_ref[...]
    over_peers(lambda peer: pattern_copy(scen, peer).start())

    @pl.when(link == 0)
    def _():
        over_peers(lambda peer: share_copy(peer, peer).wait_recv())
        corner_ref[...] = shares_ref[0]

        @pl.loop(1, scen_count)
        def _(source):
            corner_ref[...] += shares_ref[source]

        for target in range(1, link_count):
            corner_copy(target).start()

    pieces = [(scenario, piece) for scenario in range(scen_here) for piece in range(halves)]
    for scenario, piece in pieces:
        slab_copy(1, scenario, piece, across, across).wait_recv()
        slab_copy(2, scenario, piece, across, twin).start()
    beyond = lax.rem(twin + half, link_count)
    for scenario, piece in pieces:
        slab_copy(0, scenario, piece, twin, twin).wait_recv()
        slab_copy(2, scenario, piece, beyond, twin).wait_recv()
    for scenario, piece in pieces:
        slab_copy(0, scenario, piece, link, twin).wait_send()
        slab_copy(1, scenario, piece, link, across).wait_send()
        slab_copy(2, scenario, piece, across, twin).wait_send()

    @pl.when(link == 0)
    def _():
        over_peers(lambda peer: share_copy(scen, peer).wait_send())
        for target in range(1, link_count):
            corner_copy(target).wait_send()

    for scenario in range(scen_here):
        keep(scenario).wait()

    def finish_pattern(peer):
        pattern_copy(scen, peer).wait_send()
        pattern_copy(peer, peer).wait_recv()

    over_peers(finish_pattern)

    @pl.when(link != 0)
    def _():
        corner_copy(0).wait_recv()


def gather(factor_inv, coupling, diag, pattern, scen_count, link_count):
    tile = diag.shape[1]
    dma = pltpu.SemaphoreType.DMA
    pieces = (3, coupling.shape[0], 2)
    return pl.pallas_call(
        lambda *refs: gather_kernel(scen_count, link_count, *refs),
        out_shape=(
            jax.ShapeDtypeStruct((link_count,) + coupling.shape, BF16),
            jax.ShapeDtypeStruct((tile, tile), F32),
            jax.ShapeDtypeStruct((scen_count,) + pattern.shape, I32),
        ),
        in_specs=[ANY, ANY, ANY, VMEM],
        out_specs=(ANY, VMEM, VMEM),
        scratch_shapes=[
            pltpu.VMEM(factor_inv.shape, BF16),
            pltpu.VMEM(coupling.shape, BF16),
            pltpu.VMEM(diag.shape, F32),
            pltpu.VMEM(coupling.shape, BF16),
            pltpu.VMEM((scen_count, tile, tile), F32),
            dma((3, coupling.shape[0])),
            dma((coupling.shape[0],)),
            dma((2, scen_count)),
            dma((2, scen_count)),
            dma(pieces),
            dma(pieces),
            dma((link_count,)),
            dma,
        ],
        name="gather",
        compiler_params=pltpu.CompilerParams(
            collective_id=0, has_side_effects=True, vmem_limit_bytes=60 * MIB
        ),
    )(factor_inv, coupling, diag, pattern)


def contribute_kernel(
    limit, clear, target_ref, link_ref, rows_ref, own_ref, coded_ref, scales_ref
):
    scenario, piece = pl.program_id(0), pl.program_id(1)
    tile = coded_ref.shape[3]
    slots = coded_ref.shape[1]
    spread = slots * pl.num_programs(1)
    if clear:

        @pl.when((scenario == 0) & (piece == 0))
        def _():
            coded_ref[...] = jnp.zeros_like(coded_ref)
            scales_ref[...] = jnp.zeros_like(scales_ref)

    product = lax.dot_general(
        rows_ref[0, 0], own_ref[0, 0], (((0,), (0,)), ((), ())), preferred_element_type=F32
    )
    for slab in range(slots):
        values = product[slab * tile : (slab + 1) * tile]
        target = target_ref[scenario * spread + piece * slots + slab]
        dest = target // limit
        rank = target - dest * limit
        peak = jnp.max(jnp.abs(values), axis=0, keepdims=True)
        gain = jnp.where(peak > 1e-30, LEVELS / jnp.maximum(peak, 1e-30), 0.0)
        code = jnp.round(values * gain).astype(I32).astype(I16)
        scales_ref[dest, pl.ds(rank, 1), :] = peak * (1.0 / LEVELS)
        for slot in range(slots):
            coded_ref[dest, slot, pl.ds(pl.multiple_of(rank * tile, tile), tile), :] = code[
                :, slot * tile : (slot + 1) * tile
            ]


def contribute(target, link, gathered, tile, scen_count, limit):
    link_count, scen_here, depth, width = gathered.shape
    slots = width // tile
    clear = scen_count * limit > target.shape[0]
    return pl.pallas_call(
        lambda *refs: contribute_kernel(limit, clear, *refs),
        grid_spec=pltpu.PrefetchScalarGridSpec(
            num_scalar_prefetch=2,
            grid=(scen_here, link_count),
            in_specs=[
                pl.BlockSpec((1, 1, depth, width), lambda i, j, *_: (j, i, 0, 0)),
                pl.BlockSpec((1, 1, depth, width), lambda i, j, _, link: (link[0], i, 0, 0)),
            ],
            out_specs=[
                pl.BlockSpec((scen_count, slots, limit * tile, tile), lambda i, j, *_: (0, 0, 0, 0)),
                pl.BlockSpec((scen_count, 8, width), lambda i, j, *_: (0, 0, 0)),
            ],
        ),
        out_shape=(
            jax.ShapeDtypeStruct((scen_count, slots, limit * tile, tile), I16),
            jax.ShapeDtypeStruct((scen_count, 8, width), F32),
        ),
        name="contribute",
        compiler_params=pltpu.CompilerParams(vmem_limit_bytes=32 * MIB),
    )(target, link, gathered, gathered)


def exchange_kernel(
    scen_count,
    link_count,
    coded_ref,
    scales_ref,
    corner_ref,
    arrived_ref,
    arrived_scales_ref,
    lower_ref,
    side_ref,
    down_ref,
    inverse_ref,
    lead_ref,
    lead_scales_ref,
    column_ref,
    column_scales_ref,
    send_sem,
    recv_sem,
    local_sem,
    lead_send,
    lead_recv,
    link_send,
    link_recv,
):
    scen, link = lax.axis_index("scen"), lax.axis_index("link")
    tile = coded_ref.shape[3]
    slots = coded_ref.shape[1]
    greet(scen_count, link_count)

    def ends(kind, source, dest):
        if kind == 0:
            return scales_ref.at[dest], arrived_scales_ref.at[source]
        return coded_ref.at[dest, kind - 1], arrived_ref.at[source, kind - 1]

    def copy(kind, source, peer):
        src, dst = ends(kind, source, peer)
        return pltpu.make_async_remote_copy(
            src_ref=src,
            dst_ref=dst,
            send_sem=send_sem.at[kind, peer],
            recv_sem=recv_sem.at[kind, source],
            device_id={"scen": peer},
            device_id_type=MESH,
        )

    def keep(kind):
        src, dst = ends(kind, scen, scen)
        return pltpu.make_async_copy(src, dst, local_sem.at[kind])

    def over_peers(act):
        @pl.loop(1, scen_count)
        def _(step):
            act(lax.rem(scen + step, scen_count))

    first, later = (0, 1), tuple(range(2, slots + 1))

    def start_first(peer):
        for kind in first:
            copy(kind, scen, peer).start()

    def start_later(peer):
        for kind in later:
            copy(kind, scen, peer).start()

    def finish_send(kinds):
        def act(peer):
            for kind in kinds:
                copy(kind, scen, peer).wait_send()

        return act

    def finish_recv(kinds):
        def act(peer):
            for kind in kinds:
                copy(kind, peer, peer).wait_recv()

        return act

    line = scen_count // 2
    spot, side = scen // 2, lax.rem(scen, 2)
    pair = scen + 1 - 2 * side

    def lead_copies(way, block, target):
        return [
            pltpu.make_async_remote_copy(
                src_ref=ref.at[block],
                dst_ref=ref.at[block],
                send_sem=lead_send.at[which, way, block],
                recv_sem=lead_recv.at[which, block],
                device_id={"scen": target},
                device_id_type=MESH,
            )
            for which, ref in enumerate((lead_ref, lead_scales_ref))
        ]

    def lead_wait(block):
        for one in lead_copies(2, block, pair):
            one.wait_recv()

    def lead_pass(block, left, right, act):
        @pl.when(left & (spot > 0))
        def _():
            for one in lead_copies(0, block, lax.rem(scen + scen_count - 2, scen_count)):
                act(one)

        @pl.when(right & (spot < line - 1))
        def _():
            for one in lead_copies(1, block, lax.rem(scen + 2, scen_count)):
                act(one)

        for one in lead_copies(2, block, pair):
            act(one)

    def begin(one):
        one.start()

    def end(one):
        one.wait_send()

    def over_line(act, arriving):
        @pl.loop(1, line)
        def _(step):
            @pl.when(spot - step >= 0)
            def _():
                block = scen - 2 * step
                if arriving:
                    lead_wait(block)
                lead_pass(block, False, True, act)

            @pl.when(spot + step < line)
            def _():
                block = scen + 2 * step
                if arriving:
                    lead_wait(block)
                lead_pass(block, True, False, act)

    lead_ref[scen] = coded_ref[0, :, :tile, :]
    lead_scales_ref[scen] = scales_ref[0]
    lead_pass(scen, True, True, begin)
    over_peers(start_first)
    for kind in first + later:
        keep(kind).start()
    factor_into(corner_ref, lower_ref, inverse_ref)
    over_peers(finish_send(first))
    for kind in first + later:
        keep(kind).wait()

    half = link_count // 2

    def column_copies(source, target, way, relayed):
        pairs = (
            (column_ref if relayed else arrived_ref.at[:, 0], column_ref),
            (column_scales_ref if relayed else arrived_scales_ref, column_scales_ref),
        )
        return [
            pltpu.make_async_remote_copy(
                src_ref=src.at[source],
                dst_ref=dst.at[source],
                send_sem=link_send.at[which, way, source],
                recv_sem=link_recv.at[which, source],
                device_id={"link": target},
                device_id_type=MESH,
            )
            for which, (src, dst) in enumerate(pairs)
        ]

    def column_out(source):
        for target in (half,) + tuple(range(1, half)):
            for one in column_copies(source, target, target % half, False):
                one.start()

    def column_out_end(source):
        for target in (half,) + tuple(range(1, half)):
            for one in column_copies(source, target, target % half, False):
                one.wait_send()

    @pl.when(link == 0)
    def _():
        column_out(scen)

        @pl.loop(1, scen_count)
        def _(step):
            peer = lax.rem(scen + step, scen_count)
            finish_recv(first)(peer)
            column_out(peer)

    over_line(begin, True)
    over_peers(start_later)

    @pl.when(link == 0)
    def _():
        column_ref[...] = arrived_ref[:, 0]
        column_scales_ref[...] = arrived_scales_ref[...]

        @pl.loop(0, scen_count)
        def _(source):
            column_out_end(source)

    @pl.when(link != 0)
    def _():
        over_peers(finish_recv(first))

        @pl.loop(0, scen_count)
        def _(step):
            source = lax.rem(scen + step, scen_count)
            for one in column_copies(source, 0, 0, True):
                one.wait_recv()

            @pl.when(link == half)
            def _():
                for target in range(half + 1, link_count):
                    for one in column_copies(source, target, target - half, True):
                        one.start()

        @pl.when(link == half)
        def _():
            @pl.loop(0, scen_count)
            def _(source):
                for target in range(half + 1, link_count):
                    for one in column_copies(source, target, target - half, True):
                        one.wait_send()

    @pl.loop(0, line)
    def _(step):
        lead_wait(2 * step + 1 - side)

    @pl.loop(0, scen_count)
    def _(source):
        for slot in range(slots):
            at = slice(slot * tile, (slot + 1) * tile)
            side_ref[source, slot] = jnp.dot(
                inverse_ref[...],
                lead_ref[source, slot].astype(I32).astype(F32) * lead_scales_ref[source, 0:1, at],
                precision=HIGHEST,
                preferred_element_type=F32,
            )
        for rank in range(column_ref.shape[1] // tile):
            at = slice(rank * tile, (rank + 1) * tile)
            codes = column_ref[source, at, :].astype(I32).astype(F32)
            down_ref[source, at, :] = lax.dot_general(
                codes * column_scales_ref[source, rank : rank + 1, :tile],
                inverse_ref[...],
                (((1,), (1,)), ((), ())),
                precision=HIGHEST,
                preferred_element_type=F32,
            )

    lead_pass(scen, True, True, end)
    over_line(end, False)
    over_peers(finish_recv(later))
    over_peers(finish_send(later))


def exchange(coded, scales, corner, link_count):
    tile = corner.shape[0]
    scen_count, slots, rows = coded.shape[:3]
    kinds = slots + 1
    dma = pltpu.SemaphoreType.DMA
    return pl.pallas_call(
        lambda *refs: exchange_kernel(scen_count, link_count, *refs),
        out_shape=(
            jax.ShapeDtypeStruct(coded.shape, I16),
            jax.ShapeDtypeStruct(scales.shape, F32),
            jax.ShapeDtypeStruct((tile, tile), F32),
            jax.ShapeDtypeStruct((scen_count, slots, tile, tile), F32),
            jax.ShapeDtypeStruct((scen_count, rows, tile), F32),
        ),
        in_specs=[VMEM, VMEM, VMEM],
        out_specs=(VMEM,) * 5,
        scratch_shapes=[
            pltpu.VMEM((tile, tile), F32),
            pltpu.VMEM((scen_count, slots, tile, tile), I16),
            pltpu.VMEM(scales.shape, F32),
            pltpu.VMEM((scen_count, rows, tile), I16),
            pltpu.VMEM(scales.shape, F32),
            dma((kinds, scen_count)),
            dma((kinds, scen_count)),
            dma((kinds,)),
            dma((2, 3, scen_count)),
            dma((2, scen_count)),
            dma((2, max(1, link_count // 2), scen_count)),
            dma((2, scen_count)),
        ],
        name="exchange",
        compiler_params=pltpu.CompilerParams(
            collective_id=1, has_side_effects=True, vmem_limit_bytes=48 * MIB
        ),
    )(coded, scales, corner)


def split(value):
    high = value.astype(BF16)
    return high, (value - high.astype(F32)).astype(BF16)


def finish_kernel(
    limit,
    place_ref,
    row_label_ref,
    col_label_ref,
    lead_label_ref,
    column_label_ref,
    arrived_ref,
    scales_ref,
    lower_ref,
    side_ref,
    down_ref,
    diag_ref,
    panel_ref,
    trailing_ref,
    left_ref,
    raw_ref,
    list_ref,
    count_ref,
):
    tile = lower_ref.shape[0]
    chunk = trailing_ref.shape[1]
    slots = arrived_ref.shape[1]
    rows_own = diag_ref.shape[0]
    step = pl.program_id(0)
    per_chunk = chunk // tile
    scen, link = place_ref[0], place_ref[1]
    first_col = link * per_chunk * pl.num_programs(0)

    @pl.when(step == 0)
    def _():
        raw_ref[...] = jnp.zeros_like(raw_ref)
        panel_ref[...] = jnp.zeros_like(panel_ref)

        @pl.loop(0, side_ref.shape[0])
        def _(source):
            for slot in range(slots):
                at = pl.multiple_of(lead_label_ref[source * slots + slot] * tile, tile)
                raw_ref[:, pl.ds(at, tile)] += side_ref[source, slot]
            for rank in range(limit):
                label = column_label_ref[source * limit + rank]

                @pl.when(label >= 0)
                def _():
                    at = pl.ds(pl.multiple_of(label * tile, tile), tile)
                    panel_ref[at, :] += down_ref[source, rank * tile : (rank + 1) * tile, :]

        @pl.when(link == 0)
        def _():
            raw_ref[:, :tile] = lower_ref[...].T

        @pl.when(scen == 0)
        def _():
            panel_ref[:tile, :] = lower_ref[...]

        high, low = split(-panel_ref[...])
        left_ref[:, :tile] = high
        left_ref[:, tile : 2 * tile] = low
        left_ref[:, 2 * tile :] = high

        for other in range(count_ref.shape[0]):
            count_ref[other] = 0

        @pl.loop(0, list_ref.shape[1])
        def _(entry):
            @pl.when(row_label_ref[entry // slots] >= 0)
            def _():
                owner = col_label_ref[entry] // per_chunk
                held = count_ref[owner]
                list_ref[owner, held] = entry
                count_ref[owner] = held + 1

    part = raw_ref[:, pl.ds(pl.multiple_of(step * chunk, chunk), chunk)]
    high, low = split(part)
    right = jnp.concatenate([high, high, low], axis=0)
    strip = min(8, rows_own) * tile
    for at in range(0, rows_own * tile, strip):
        trailing_ref[at : at + strip, :] = jnp.dot(
            left_ref[at : at + strip, :], right, preferred_element_type=F32
        )

    @pl.loop(0, count_ref[step])
    def _(place):
        entry = list_ref[step, place]
        listed = entry // slots
        slot = entry - listed * slots
        source = listed // limit
        rank = listed - source * limit
        col = col_label_ref[entry] - step * per_chunk
        down = pl.ds(pl.multiple_of(row_label_ref[listed] * tile, tile), tile)
        along = pl.ds(pl.multiple_of(col * tile, tile), tile)
        from_rows = pl.ds(pl.multiple_of(rank * tile, tile), tile)
        from_lanes = pl.ds(pl.multiple_of(slot * tile, tile), tile)
        scales = scales_ref[source, :, from_lanes]
        picked = lax.broadcasted_iota(I32, scales.shape, 0) == rank
        scale = jnp.sum(jnp.where(picked, scales, 0.0), axis=0, keepdims=True)
        codes = arrived_ref[source, slot, from_rows, :]
        trailing_ref[down, along] += codes.astype(I32).astype(F32) * scale

    unit = lax.broadcasted_iota(I32, (tile, tile), 0) == lax.broadcasted_iota(
        I32, (tile, tile), 1
    )
    for col in range(per_chunk):
        row = first_col + step * per_chunk + col - scen * rows_own

        @pl.when((row >= 0) & (row < rows_own))
        def _():
            down = pl.ds(pl.multiple_of(row * tile, tile), tile)
            trailing_ref[down, col * tile : (col + 1) * tile] += jnp.where(
                unit, diag_ref[pl.ds(row, 1), :], 0.0
            )


def finish(labels, arrays, limit, width):
    lower, diag = arrays[2], arrays[5]
    entries = labels[2].shape[0]
    tile = lower.shape[0]
    rows = diag.shape[0] * tile
    chunk = min(512, width)
    return pl.pallas_call(
        lambda *refs: finish_kernel(limit, *refs),
        grid_spec=pltpu.PrefetchScalarGridSpec(
            num_scalar_prefetch=5,
            grid=(width // chunk,),
            in_specs=[VMEM] * len(arrays),
            out_specs=[
                pl.BlockSpec((rows, tile), lambda c, *_: (0, 0)),
                pl.BlockSpec((rows, chunk), lambda c, *_: (0, c)),
            ],
            scratch_shapes=[
                pltpu.VMEM((rows, 3 * tile), BF16),
                pltpu.VMEM((tile, width), F32),
                pltpu.SMEM((width // chunk, entries), I32),
                pltpu.SMEM((width // chunk,), I32),
            ],
        ),
        out_shape=(
            jax.ShapeDtypeStruct((rows, tile), F32),
            jax.ShapeDtypeStruct((rows, width), F32),
        ),
        name="finish",
        compiler_params=pltpu.CompilerParams(vmem_limit_bytes=48 * MIB),
    )(*labels, *arrays)


def per_device(factor_inv, coupling, first_diag, pattern):
    rows_own, tile = first_diag.shape
    scen_count = lax.axis_size("scen")
    link_count = lax.axis_size("link")
    scen_pos = lax.axis_index("scen")
    link_pos = lax.axis_index("link")
    per_link = rows_own * scen_count // link_count
    scen_here, spread = pattern.shape
    width = coupling.shape[2]
    slots = width // tile

    padded = jnp.pad(pattern, ((0, 8 - scen_here), (0, 128 - spread)))
    gathered, corner, patterns = gather(
        factor_inv, coupling, first_diag, padded, scen_count, link_count
    )
    patterns = patterns[:, :scen_here, :spread]

    picks = scen_here * slots
    owners_here = max(1, per_link // rows_own)
    limit = max(1, (picks + owners_here - 1) // owners_here)
    listed = jnp.arange(scen_here * spread, dtype=I32)

    def targets(blocks):
        owners = blocks // rows_own
        earlier = (owners[..., :, None] == owners[..., None, :]) & (
            listed[None, :] < listed[:, None]
        )
        return owners * limit + jnp.sum(earlier.astype(I32), axis=-1)

    coded, scales = contribute(
        targets(pattern.reshape(-1)), link_pos[None].astype(I32), gathered, tile, scen_count, limit
    )

    blocks = patterns.reshape(scen_count, scen_here * spread)
    places = scen_pos * limit + jnp.arange(limit, dtype=I32)
    hit = targets(blocks)[:, :, None] == places[None, None, :]
    rows_from = blocks - scen_pos * rows_own + 1
    row_labels = jnp.sum(jnp.where(hit, rows_from[:, :, None], 0), axis=1) - 1
    leading = jnp.repeat(patterns[:, :, 0] == 0, spread, axis=1)
    column_labels = (
        jnp.sum(jnp.where(hit & leading[:, :, None], rows_from[:, :, None], 0), axis=1) - 1
    )
    own_cols = (
        lax.dynamic_slice_in_dim(patterns, link_pos * slots, slots, 2) - link_pos * per_link
    )
    slab_cols = jnp.repeat(own_cols, spread, axis=1)
    col_labels = jnp.sum(jnp.where(hit[:, :, :, None], slab_cols[:, :, None, :], 0), axis=1)
    lead_labels = own_cols[:, 0, :]

    arrays = exchange(coded, scales, corner, link_count) + (first_diag,)
    place = jnp.stack([scen_pos, link_pos]).astype(I32)
    labels = (place,) + tuple(
        one.reshape(-1) for one in (row_labels, col_labels, lead_labels, column_labels)
    )
    return finish(labels, arrays, limit, per_link * tile)


def solution(mesh):
    in_specs = (P("scen", None, None), P("scen", None, "link"), P("scen", None), P("scen", None))
    out_specs = (P("scen", None), P("scen", "link"))
    return jax.shard_map(
        per_device, mesh=mesh, in_specs=in_specs, out_specs=out_specs, check_vma=False
    )
```
